32 devices in a mesh: member: 2 (over core), rep: 4 (over z), tensor: 4 (over y, x).
Axes of the slice: x: 2, y: 2, z: 4, core: 2. Of those that a mesh axis runs over, the one named last changes fastest.
Arguments:
- queries: bfloat16 [2, 32, 32, 128], P('member', 'rep'), parts along dimension 1, may hold values from -110 to 110
- keys: bfloat16 [2, 32, 8192, 128], P('member', 'rep', 'tensor'), parts along dimension 1, may hold values from -4.2 to 4.2
- values: bfloat16 [2, 32, 8192, 128], P('member', 'rep', 'tensor'), parts along dimension 1, may hold values from -6 to 6
- lengths: int32 [32], P('rep'), parts along dimension 0, may hold values from 256 to 2048, as said below
- targets: int32 [32], P('rep'), parts along dimension 0, may hold values from 0 to 4095
- residual: bfloat16 [2, 32, 4096], P('member', 'rep'), parts along dimension 1, may hold values from -32 to 32
- out_weight: bfloat16 [2, 4096, 4096], P('member', 'tensor'), may hold values from -0.75 to 0.75
- norm_gain: float32 [2, 4096], P('member'), may hold values from 0.5 to 1.5
- head_weight: bfloat16 [2, 4096, 4096], P('member', None, 'tensor'), may hold values from -0.2 to 0.2878906
Outputs:
- mean_logprobs: float32 [32, 4096], P(('rep', 'member'), 'tensor'), parts along dimension 0
- target_logprob: float32 [32], P(('rep', 'member')), parts along dimension 0
The draws below stay inside these ranges and needn't reach their ends.
There are 4 independent parts, one for each index of `rep`. The reference program is written for one: setup_inputs(seed, part) draws one part's arguments, and reference() takes and returns one part's arrays. A program takes and returns all parts, laid end to end along the dimension named above; an argument that names none is the same for every part. Nothing has to cross between parts.
Inputs may be any that keep to these rules, and one draw needn't show every extreme that they name: `lengths`: some row of every draw has all 2048 slots live.
All inputs are finite; a program needn't handle non-finite values.
Results may differ from the reference program's by a relative error of at most 0.004.
Values may be sent and summed in bfloat16 or wider, within the bound.
No kernel may reach another device: no remote copies, remote signals or barrier semaphores. Data moves between devices by JAX's collectives and lax.ppermute only.
A program may use at most 64 MiB of HBM per device.

```python
import jax
import jax.numpy as jnp
from jax import lax

D = 4096
HEADS = 32
KV_HEADS = 4
HEAD_DIM = 128
CTX = 2048
ROWS = 8
VOCAB = 4096


def joint_draw(key):
    per_kv = HEADS // KV_HEADS
    key_query = jax.random.fold_in(key, 11)
    key_cache = jax.random.fold_in(key, 12)
    cache = jax.random.truncated_normal(key_cache, -4.0, 4.0, (2, ROWS, KV_HEADS, CTX, HEAD_DIM), jnp.float32)
    query_draw = jax.random.truncated_normal(key_query, -4.0, 4.0, (2, ROWS, KV_HEADS, per_kv, HEAD_DIM), jnp.float32)
    return (query_draw.reshape(2, ROWS, HEADS, HEAD_DIM), cache.reshape(2, ROWS, KV_HEADS * CTX, HEAD_DIM))


def draw_queries(key, part):
    return joint_draw(key)[0].astype(jnp.bfloat16)


def draw_keys(key, part):
    return joint_draw(key)[1].astype(jnp.bfloat16)


def draw_lengths(key, part):
    key_len = jax.random.fold_in(key, 21)
    key_row = jax.random.fold_in(key, 22)
    drawn = jax.random.randint(key_len, (ROWS,), CTX // 8, CTX + 1)
    full_row = jax.random.randint(key_row, (), 0, ROWS)
    return jnp.where(jnp.arange(ROWS, dtype=jnp.int32) == full_row, CTX, drawn).astype(jnp.int32)


def draw_residual(key, part):
    stream = 0.3 * jax.random.truncated_normal(jax.random.fold_in(key, 31), -4.0, 4.0, (2, ROWS, D), jnp.float32)
    return stream.astype(jnp.bfloat16)


def draw_head_weight(key, part):
    matrix = jax.random.truncated_normal(jax.random.fold_in(key, 41), -4.0, 4.0, (2, D, VOCAB), jnp.float32)
    matrix = matrix * (1.0 / 450.0 ** 0.5)
    return matrix.astype(jnp.bfloat16)


def touch_ends(values, own_key, low, largest):
    spot = [jax.random.randint(jax.random.fold_in(own_key, axis), (), 0, length) for axis, length in enumerate(values.shape)]
    main_axis = values.shape.index(max(values.shape))
    neighbour = spot[:main_axis] + [(spot[main_axis] + 1) % values.shape[main_axis]] + spot[main_axis + 1:]
    return values.at[tuple(spot)].set(low).at[tuple(neighbour)].set(largest)


def level_of(key, shape, shards, least, largest):
    def one(dim, parts):
        heights = jax.random.uniform(jax.random.fold_in(jax.random.fold_in(key, 6), dim), (parts,), jnp.float32, least / len(shards), largest / len(shards))
        return jnp.repeat(jnp.exp(heights), shape[dim] // parts).reshape((-1,) + (1,) * (len(shape) - dim - 1))

    factor_of = one(*shards[0])
    for cut in shards[1:]:
        factor_of = factor_of * one(*cut)
    return factor_of


def scatter_about(key, dims, spread, bound, cuts=(), kind=jnp.bfloat16):
    result = spread * jax.random.normal(key, dims, jnp.float32)
    if cuts:
        result = result * level_of(key, dims, cuts, -0.22, 0.18)
    return jnp.clip(result, -bound, bound).astype(kind)


def setup_inputs(seed: int = 0, part: int = 0) -> dict:
    streams_of = jax.random.split(jax.random.key(seed), 10)
    part_keys = jax.random.split(jax.random.fold_in(streams_of[9], part), 10)
    queries = draw_queries(jax.random.fold_in(jax.random.fold_in(streams_of[9], part), 71), part)
    keys = draw_keys(jax.random.fold_in(jax.random.fold_in(streams_of[9], part), 71), part)
    values = scatter_about(part_keys[2], (2, ROWS, KV_HEADS * CTX, HEAD_DIM), 1.0, 6.0, ((0, 2), (2, 4)))
    lengths = draw_lengths(jax.random.fold_in(jax.random.fold_in(streams_of[9], part), 71), part)
    targets = touch_ends(jax.random.randint(part_keys[4], (ROWS,), 0, VOCAB), jax.random.fold_in(part_keys[4], 1), 0, VOCAB - 1).astype(jnp.int32)
    residual = draw_residual(jax.random.fold_in(jax.random.fold_in(streams_of[9], part), 71), part)
    out_weight = scatter_about(streams_of[6], (2, HEADS * HEAD_DIM, D), 64 ** -0.5, 0.75, ((0, 2), (1, 4)))
    norm_gain = jnp.clip(1.0 + 0.1 * jax.random.normal(streams_of[7], (2, D), jnp.float32), 0.5, 1.5)
    head_weight = draw_head_weight(jax.random.fold_in(streams_of[9], 71), part)
    return dict(queries=queries, keys=keys, values=values, lengths=lengths, targets=targets, residual=residual, out_weight=out_weight, norm_gain=norm_gain, head_weight=head_weight)


def reference(queries, keys, values, lengths, targets, residual, out_weight, norm_gain, head_weight):
    per_kv = HEADS // KV_HEADS
    slot_pos = jnp.arange(CTX, dtype=jnp.int32)
    live = (slot_pos[None, :] < lengths[:, None])[:, None, None, :]
    scale_factor = 1.0 / HEAD_DIM ** 0.5
    results = []
    for member in range(2):
        query_all = queries[member].astype(jnp.float32).reshape(ROWS, KV_HEADS, per_kv, HEAD_DIM)
        key_all = keys[member].astype(jnp.float32).reshape(ROWS, KV_HEADS, CTX, HEAD_DIM)
        value_all = values[member].astype(jnp.float32).reshape(ROWS, KV_HEADS, CTX, HEAD_DIM)
        scores = jnp.einsum('rgqd,rgcd->rgqc', query_all, key_all) * scale_factor
        scores = jnp.where(live, scores, jnp.float32(-1e+30))
        top_score = lax.optimization_barrier(jnp.max(scores, axis=-1))
        weights = jnp.where(live, jnp.exp(scores - top_score[..., None]), jnp.float32(0.0))
        weight_total = lax.optimization_barrier(jnp.sum(weights, axis=-1))
        rounded = lax.optimization_barrier(weights.astype(jnp.bfloat16)).astype(jnp.float32)
        weighted = jnp.einsum('rgqc,rgcd->rgqd', rounded, value_all)
        attended = (weighted / weight_total[..., None]).reshape(ROWS, HEADS * HEAD_DIM).astype(jnp.bfloat16)
        projected = jnp.dot(attended, out_weight[member], preferred_element_type=jnp.float32)
        hidden = residual[member].astype(jnp.float32) + projected
        normed = hidden * lax.rsqrt(lax.optimization_barrier(jnp.mean(hidden * hidden, axis=-1, keepdims=True)) + 1e-05) * norm_gain[member]
        normed = normed.astype(jnp.bfloat16)
        logits = jnp.dot(normed, head_weight[member], preferred_element_type=jnp.float32)
        top_logit = lax.optimization_barrier(jnp.max(logits, axis=-1, keepdims=True))
        log_total = top_logit + jnp.log(lax.optimization_barrier(jnp.sum(jnp.exp(logits - top_logit), axis=-1, keepdims=True)))
        results.append(logits - log_total)
    mean_logprobs = 0.5 * (results[0] + results[1])
    target_logprob = jnp.take_along_axis(mean_logprobs, targets[:, None].astype(jnp.int32), axis=1)[:, 0]
    return (mean_logprobs, target_logprob)
```

```python
import functools

import jax
import jax.numpy as jnp
from jax import lax
from jax.experimental import pallas as pl
from jax.experimental.pallas import tpu as pltpu
from jax.sharding import PartitionSpec as P

HEADS = 32
KV_HEADS = 4
SLOT_BLOCK = 512
LEAST_LIVE = 256
STAT_LANES = 128
f32 = jnp.float32
bf16 = jnp.bfloat16


def for_sending(shard):

    def short(part):
        return part.astype(jnp.bfloat16) if part.dtype == jnp.float32 else part

    return jax.tree.map(short, shard)


def swapped(block, axis, distance):
    count = lax.axis_size(axis)
    route = []
    for low in range(count):
        high = low | 1 << distance
        if high != low and high < count:
            route += [(low, high), (high, low)]
    return lax.ppermute(block, axis, route)


def crossed(block, axis, mask):
    count = lax.axis_size(axis)
    return lax.ppermute(block, axis, [(i, i ^ mask) for i in range(count)])


def join_partial(earlier, later):
    peak_one, total_one, weighted_one = earlier
    peak_two, total_two, weighted_two = later
    peak_new = jnp.maximum(peak_one, peak_two)
    scale_one = jnp.exp(peak_one - peak_new)
    scale_two = jnp.exp(peak_two - peak_new)
    total_new = total_one * scale_one + total_two * scale_two
    weighted_new = weighted_one * scale_one[..., None] + weighted_two * scale_two[..., None]
    return (peak_new, total_new, weighted_new)


def attend_project_kernel(
    lengths, queries, keys_hbm, values_hbm, weight_hbm, out,
    keys, values, weight, query, scores, probs, heads_out, key_sem, value_sem, weight_sem,
):
    row_count, span, depth = keys_hbm.shape
    heads_kv = HEADS // KV_HEADS
    blocks = span // SLOT_BLOCK
    width = weight_hbm.shape[1]
    pieces = weight_sem.shape[0]
    piece = width // pieces

    def copy_of(source, target, sem, r, c):
        slots = pl.ds(c * SLOT_BLOCK, SLOT_BLOCK)
        return pltpu.make_async_copy(source.at[r, slots], target.at[r, slots], sem.at[r, c])

    def weight_copy(n):
        columns = pl.ds(n * piece, piece)
        return pltpu.make_async_copy(weight_hbm.at[:, columns], weight.at[:, columns], weight_sem.at[n])

    def when_live(r, c, action):
        if c * SLOT_BLOCK < LEAST_LIVE:
            action()
        else:
            pl.when(lengths[r] > c * SLOT_BLOCK)(action)

    for r in range(row_count):
        for c in range(blocks):
            when_live(r, c, lambda: copy_of(keys_hbm, keys, key_sem, r, c).start())
    for r in range(row_count):
        for c in range(blocks):
            when_live(r, c, lambda: copy_of(values_hbm, values, value_sem, r, c).start())
    for n in range(pieces):
        weight_copy(n).start()

    for r in range(row_count):
        for c in range(blocks):
            if c * SLOT_BLOCK >= LEAST_LIVE:

                @pl.when(lengths[r] <= c * SLOT_BLOCK)
                def _():
                    values[r, c * SLOT_BLOCK : (c + 1) * SLOT_BLOCK] = jnp.zeros((SLOT_BLOCK, depth), bf16)

    query[...] = queries[...].astype(f32)
    first_head = pl.multiple_of(lax.axis_index("tensor") * heads_kv, heads_kv)
    for r in range(row_count):
        for c in range(blocks):
            when_live(r, c, lambda: copy_of(keys_hbm, keys, key_sem, r, c).wait())
        own = query[r, pl.ds(first_head, heads_kv), :].astype(bf16)
        score = lax.dot_general(own, keys[r], (((1,), (1,)), ((), ())), preferred_element_type=f32)
        score = score * (1.0 / depth**0.5)
        slot = lax.broadcasted_iota(jnp.int32, score.shape, 1)
        scores[r * heads_kv : (r + 1) * heads_kv] = jnp.where(slot < lengths[r], score, -1e30)
    totals = []
    for r in range(row_count):
        rows = slice(r * heads_kv, (r + 1) * heads_kv)
        score = scores[rows]
        top = jnp.max(score, axis=1, keepdims=True)
        slot = lax.broadcasted_iota(jnp.int32, score.shape, 1)
        mass = jnp.where(slot < lengths[r], jnp.exp(score - top), 0.0)
        totals.append(jnp.sum(mass, axis=1, keepdims=True))
        probs[r] = mass.astype(bf16)
    for r in range(row_count):
        for c in range(blocks):
            when_live(r, c, lambda: copy_of(values_hbm, values, value_sem, r, c).wait())
        mixed = jnp.dot(probs[r], values[r], preferred_element_type=f32)
        heads_out[r * heads_kv : (r + 1) * heads_kv] = mixed / totals[r]
    attended = jnp.concatenate(
        [heads_out[pl.ds(h, row_count, stride=heads_kv), :] for h in range(heads_kv)], axis=1
    ).astype(bf16)
    for n in range(pieces):
        weight_copy(n).wait()
        columns = slice(n * piece, (n + 1) * piece)
        out[:, columns] = jnp.dot(attended, weight[:, columns], preferred_element_type=f32).astype(out.dtype)


def attend_project(lengths, queries, keys, values, weight):
    row_count, span, depth = keys.shape
    heads_kv = HEADS // KV_HEADS
    width = weight.shape[1]
    pieces = 8
    blocks = span // SLOT_BLOCK
    vmem = pl.BlockSpec(memory_space=pltpu.VMEM)
    hbm = pl.BlockSpec(memory_space=pl.ANY)
    return pl.pallas_call(
        attend_project_kernel,
        out_shape=jax.ShapeDtypeStruct((row_count, width), bf16),
        in_specs=[pl.BlockSpec(memory_space=pltpu.SMEM), vmem, hbm, hbm, hbm],
        out_specs=vmem,
        scratch_shapes=[
            pltpu.VMEM(keys.shape, bf16),
            pltpu.VMEM(values.shape, bf16),
            pltpu.VMEM(weight.shape, bf16),
            pltpu.VMEM(queries.shape, f32),
            pltpu.VMEM((row_count * heads_kv, span), f32),
            pltpu.VMEM((row_count, heads_kv, span), bf16),
            pltpu.VMEM((row_count * heads_kv, depth), f32),
            pltpu.SemaphoreType.DMA((row_count, blocks)),
            pltpu.SemaphoreType.DMA((row_count, blocks)),
            pltpu.SemaphoreType.DMA((pieces,)),
        ],
        compiler_params=pltpu.CompilerParams(vmem_limit_bytes=60 << 20),
        name="attend_project",
    )(lengths, queries, keys, values, weight)


def head_kernel(part_count, targets, *refs):
    parts = refs[:part_count]
    residual, gain, weight, keep, send = refs[part_count:]
    row_count, width = residual.shape
    vocab = weight.shape[1]
    half = row_count // 2
    hidden = residual[...].astype(f32)
    for part in parts:
        hidden = hidden + part[...].astype(f32)
    scale = lax.rsqrt(jnp.mean(hidden * hidden, axis=1, keepdims=True) + 1e-05)
    normed = (hidden * scale * gain[...]).astype(bf16)
    logits = jnp.dot(normed, weight[...], preferred_element_type=f32)
    row = lax.broadcasted_iota(jnp.int32, (row_count, 1), 0)
    wanted = jnp.zeros((row_count, 1), jnp.int32)
    for r in range(row_count):
        wanted = jnp.where(row == r, targets[r], wanted)
    wanted = wanted - lax.axis_index("tensor") * vocab
    entry = lax.broadcasted_iota(jnp.int32, (row_count, vocab), 1)
    pick = jnp.sum(jnp.where(entry == wanted, logits, 0.0), axis=1, keepdims=True)
    top = jnp.max(logits, axis=1, keepdims=True)
    mass = jnp.sum(jnp.exp(logits - top), axis=1, keepdims=True)
    lane = lax.broadcasted_iota(jnp.int32, (row_count, STAT_LANES), 1)
    stats = jnp.where(lane == 0, top, jnp.where(lane == 1, mass, pick))
    second = lax.axis_index("member") == 1
    for lanes, block in ((slice(0, vocab), logits), (slice(vocab, vocab + STAT_LANES), stats)):
        keep[:, lanes] = jnp.where(second, block[half:], block[:half])
        send[:, lanes] = jnp.where(second, block[:half], block[half:])


def head_rows(targets, parts, residual, gain, weight):
    row_count, width = residual.shape
    vocab = weight.shape[1]
    vmem = pl.BlockSpec(memory_space=pltpu.VMEM)
    shape = jax.ShapeDtypeStruct((row_count // 2, vocab + STAT_LANES), f32)
    return pl.pallas_call(
        functools.partial(head_kernel, len(parts)),
        out_shape=(shape, shape),
        in_specs=[pl.BlockSpec(memory_space=pltpu.SMEM)] + [vmem] * (len(parts) + 3),
        out_specs=(vmem, vmem),
        compiler_params=pltpu.CompilerParams(vmem_limit_bytes=16 << 20),
        name="head_rows",
    )(targets, *parts, residual, gain, weight)


def finish_kernel(tile_count, keep, other, *refs):
    tiles = [ref[...] for ref in refs[:tile_count]]
    mean_out, target_out = refs[tile_count:]
    half, vocab = mean_out.shape
    top = functools.reduce(jnp.maximum, [tile[:, 0:1] for tile in tiles])
    mass = sum(tile[:, 1:2] * jnp.exp(tile[:, 0:1] - top) for tile in tiles)
    pick = sum(tile[:, 2:3] for tile in tiles)
    log_total = top + jnp.log(mass)
    both = log_total[:half] + log_total[half:]
    mean_out[...] = 0.5 * ((keep[:, :vocab] + other[:, :vocab]) - both)
    target = 0.5 * ((pick[:half] + pick[half:]) - both)
    for r in range(half):
        target_out[r] = target[r, 0]


def finish(keep, other, tiles):
    half = keep.shape[0]
    vocab = keep.shape[1] - STAT_LANES
    vmem = pl.BlockSpec(memory_space=pltpu.VMEM)
    return pl.pallas_call(
        functools.partial(finish_kernel, len(tiles)),
        out_shape=(jax.ShapeDtypeStruct((half, vocab), f32), jax.ShapeDtypeStruct((half,), f32)),
        in_specs=[vmem] * (2 + len(tiles)),
        out_specs=(vmem, pl.BlockSpec(memory_space=pltpu.SMEM)),
        compiler_params=pltpu.CompilerParams(vmem_limit_bytes=4 << 20),
        name="finish",
    )(keep, other, *tiles)


def attend_shared(queries, keys, values, lengths, group_size, heads_dev):
    my_rank = lax.axis_index("tensor")
    heads_kv = HEADS // KV_HEADS
    row_count, key_span, head_depth = keys.shape
    kv_index = my_rank // group_size
    slot_first = my_rank % group_size * key_span
    group_query = lax.dynamic_slice_in_dim(queries, kv_index * heads_kv, heads_kv, 1)
    scores = jnp.einsum("rqd,rcd->rqc", group_query, keys, preferred_element_type=jnp.float32)
    scores = scores * (1.0 / head_depth**0.5)
    slot_ids = slot_first + jnp.arange(key_span, dtype=jnp.int32)
    live = (slot_ids[None, :] < lengths[:, None])[:, None, :]
    scores = jnp.where(live, scores, jnp.float32(-1e30))
    top_score = jnp.max(scores, axis=-1)
    weights = jnp.where(live, jnp.exp(scores - top_score[..., None]), jnp.float32(0.0))
    weight_total = jnp.sum(weights, axis=-1)
    weighted = jnp.einsum(
        "rqc,rcd->rqd", weights.astype(jnp.bfloat16), values, preferred_element_type=jnp.float32
    )
    state = (top_score, weight_total, weighted)
    for level in range(group_size.bit_length() - 1):
        partner = swapped(
            (for_sending(state[0]), for_sending(state[1]), for_sending(state[2])), "tensor", level
        )
        state = join_partial(state, partner)
    top_score, weight_total, weighted = state
    head_first = my_rank % group_size * heads_dev
    own_total = lax.dynamic_slice_in_dim(weight_total, head_first, heads_dev, 1)
    own_weighted = lax.dynamic_slice_in_dim(weighted, head_first, heads_dev, 1)
    return (
        (own_weighted / own_total[..., None])
        .reshape(row_count, heads_dev * head_depth)
        .astype(jnp.bfloat16)
    )


def local(queries, keys, values, lengths, targets, residual, out_weight, norm_gain, head_weight):
    axis_width = lax.axis_size("tensor")
    group_size = axis_width // KV_HEADS
    heads_dev = HEADS // axis_width
    direct = axis_width <= 4
    if group_size == 1:
        projected = attend_project(lengths, queries[0], keys[0], values[0], out_weight[0])
    else:
        attended = attend_shared(queries[0], keys[0], values[0], lengths, group_size, heads_dev)
        projected = jnp.dot(attended, out_weight[0], preferred_element_type=jnp.float32).astype(bf16)
    if direct:
        parts = [projected] + [crossed(projected, "tensor", mask) for mask in range(1, axis_width)]
    else:
        parts = [lax.psum(projected, "tensor")]
    keep, send = head_rows(targets, parts, residual[0], norm_gain, head_weight[0])
    other = swapped(send, "member", 0)
    vocab = head_weight.shape[2]
    tile = jnp.concatenate([keep[:, vocab:], other[:, vocab:]], axis=0)
    if direct:
        tiles = [tile] + [crossed(tile, "tensor", mask) for mask in range(1, axis_width)]
    else:
        gathered = lax.all_gather(tile, "tensor")
        tiles = [gathered[i] for i in range(axis_width)]
    return finish(keep, other, tiles)


def solution(mesh):
    placed = (
        P("member", "rep", None, None),
        P("member", "rep", "tensor", None),
        P("member", "rep", "tensor", None),
        P("rep"),
        P("rep"),
        P("member", "rep", None),
        P("member", "tensor", None),
        P("member", None),
        P("member", None, "tensor"),
    )
    return jax.shard_map(
        local,
        mesh=mesh,
        in_specs=placed,
        out_specs=(P(("rep", "member"), "tensor"), P(("rep", "member"))),
        check_vma=False,
    )
```

```python
import functools

import jax
import jax.numpy as jnp
from jax import lax
from jax.experimental import pallas as pl
from jax.experimental.pallas import tpu as pltpu
from jax.sharding import PartitionSpec as P

HEADS = 32
KV_HEADS = 4
SLOT_BLOCK = 128
LEAST_LIVE = 256
STAT_LANES = 128
f32 = jnp.float32
bf16 = jnp.bfloat16


def for_sending(shard):

    def short(part):
        return part.astype(jnp.bfloat16) if part.dtype == jnp.float32 else part

    return jax.tree.map(short, shard)


def swapped(block, axis, distance):
    count = lax.axis_size(axis)
    route = []
    for low in range(count):
        high = low | 1 << distance
        if high != low and high < count:
            route += [(low, high), (high, low)]
    return lax.ppermute(block, axis, route)


def crossed(block, axis, mask):
    count = lax.axis_size(axis)
    return lax.ppermute(block, axis, [(i, i ^ mask) for i in range(count)])


def join_partial(earlier, later):
    peak_one, total_one, weighted_one = earlier
    peak_two, total_two, weighted_two = later
    peak_new = jnp.maximum(peak_one, peak_two)
    scale_one = jnp.exp(peak_one - peak_new)
    scale_two = jnp.exp(peak_two - peak_new)
    total_new = total_one * scale_one + total_two * scale_two
    weighted_new = weighted_one * scale_one[..., None] + weighted_two * scale_two[..., None]
    return (peak_new, total_new, weighted_new)


def attend_project_kernel(
    lengths_hbm, queries_hbm, keys_hbm, values_hbm, weight_hbm, out,
    lengths, queries, keys, values, weight, query, scores, probs, heads_out,
    small_sem, key_sem, value_sem, weight_sem,
):
    row_count, span, depth = keys_hbm.shape
    heads_kv = HEADS // KV_HEADS
    pieces = weight_sem.shape[0]
    piece = weight_hbm.shape[0] // pieces
    half = row_count // 2
    halves = (range(half), range(half, row_count))

    def live_copy(source, target, sem, r):
        live = (lengths[r] + (SLOT_BLOCK - 1)) // SLOT_BLOCK * SLOT_BLOCK
        slots = pl.ds(0, pl.multiple_of(live, SLOT_BLOCK))
        return pltpu.make_async_copy(source.at[r, slots], target.at[r, slots], sem.at[r])

    def key_copy(r):
        return live_copy(keys_hbm, keys, key_sem, r)

    def value_copy(r):
        return live_copy(values_hbm, values, value_sem, r)

    def weight_copy(n):
        rows = pl.ds(n * piece, piece)
        return pltpu.make_async_copy(weight_hbm.at[rows], weight.at[rows], weight_sem.at[n])

    lengths_copy = pltpu.make_async_copy(lengths_hbm, lengths, small_sem.at[0])
    queries_copy = pltpu.make_async_copy(queries_hbm, queries, small_sem.at[1])
    lengths_copy.start()
    queries_copy.start()
    values[:, LEAST_LIVE:] = jnp.zeros((row_count, span - LEAST_LIVE, depth), bf16)
    lengths_copy.wait()
    for r in range(row_count):
        key_copy(r).start()
    for r in range(row_count):
        value_copy(r).start()
    queries_copy.wait()
    query[...] = queries[...].astype(f32)
    first_head = pl.multiple_of(lax.axis_index("tensor") * heads_kv, heads_kv)
    for part, rows in enumerate(halves):
        for r in rows:
            key_copy(r).wait()
        for n in range(part * pieces // 2, (part + 1) * pieces // 2):
            weight_copy(n).start()
        for r in rows:
            own = query[r, pl.ds(first_head, heads_kv), :].astype(bf16)
            score = lax.dot_general(own, keys[r], (((1,), (1,)), ((), ())), preferred_element_type=f32)
            slot = lax.broadcasted_iota(jnp.int32, score.shape, 1)
            scores[r * heads_kv : (r + 1) * heads_kv] = jnp.where(slot < lengths[r], score, -1e30)
    totals = []
    for r in range(row_count):
        score = scores[r * heads_kv : (r + 1) * heads_kv]
        top = jnp.max(score, axis=1, keepdims=True)
        mass = jnp.exp((score - top) * (1.0 / depth**0.5))
        totals.append(jnp.sum(mass, axis=1, keepdims=True))
        probs[r] = mass.astype(bf16)
    for rows in halves:
        for r in rows:
            value_copy(r).wait()
        for r in rows:
            mixed = jnp.dot(probs[r], values[r], preferred_element_type=f32)
            heads_out[r * heads_kv : (r + 1) * heads_kv] = mixed / totals[r]
    attended = jnp.concatenate(
        [heads_out[pl.ds(h, row_count, stride=heads_kv), :] for h in range(heads_kv)], axis=1
    ).astype(bf16)
    total = None
    for n in range(pieces):
        weight_copy(n).wait()
        rows = slice(n * piece, (n + 1) * piece)
        term = jnp.dot(attended[:, rows], weight[rows], preferred_element_type=f32)
        total = term if total is None else total + term
    out[...] = total.astype(out.dtype)


def in_hbm(array):
    return pltpu.with_memory_space_constraint(array, pltpu.HBM)


def attend_project(lengths, queries, keys, values, weight):
    row_count, span, depth = keys.shape
    heads_kv = HEADS // KV_HEADS
    pieces = 8
    return pl.pallas_call(
        attend_project_kernel,
        out_shape=jax.ShapeDtypeStruct((row_count, weight.shape[1]), bf16),
        in_specs=[pl.BlockSpec(memory_space=pl.ANY)] * 5,
        out_specs=pl.BlockSpec(memory_space=pltpu.VMEM),
        scratch_shapes=[
            pltpu.SMEM(lengths.shape, jnp.int32),
            pltpu.VMEM(queries.shape, bf16),
            pltpu.VMEM(keys.shape, bf16),
            pltpu.VMEM(values.shape, bf16),
            pltpu.VMEM(weight.shape, bf16),
            pltpu.VMEM(queries.shape, f32),
            pltpu.VMEM((row_count * heads_kv, span), f32),
            pltpu.VMEM((row_count, heads_kv, span), bf16),
            pltpu.VMEM((row_count * heads_kv, depth), f32),
            pltpu.SemaphoreType.DMA((2,)),
            pltpu.SemaphoreType.DMA((row_count,)),
            pltpu.SemaphoreType.DMA((row_count,)),
            pltpu.SemaphoreType.DMA((pieces,)),
        ],
        compiler_params=pltpu.CompilerParams(vmem_limit_bytes=28 << 20),
        name="attend_project",
    )(in_hbm(lengths), in_hbm(queries), in_hbm(keys), in_hbm(values), in_hbm(weight))


def fetch_kernel(after, source, target, sem):
    copies = []
    pieces = sem.shape[0]
    piece = source.shape[0] // pieces
    for n in range(pieces):
        rows = pl.ds(n * piece, piece)
        copies.append(pltpu.make_async_copy(source.at[rows], target.at[rows], sem.at[n]))
    for copy in copies:
        copy.start()
    for copy in copies:
        copy.wait()


def fetch(after, source):
    anywhere = pl.BlockSpec(memory_space=pl.ANY)
    return pl.pallas_call(
        fetch_kernel,
        out_shape=pltpu.VMEM(source.shape, source.dtype),
        in_specs=[anywhere, anywhere],
        out_specs=anywhere,
        scratch_shapes=[pltpu.SemaphoreType.DMA((4,))],
        compiler_params=pltpu.CompilerParams(vmem_limit_bytes=1 << 20),
        cost_estimate=pl.CostEstimate(flops=0, bytes_accessed=2 * source.size * source.dtype.itemsize, transcendentals=0),
        name="fetch",
    )(after, in_hbm(source))


def head_kernel(part_count, targets, *refs):
    parts = refs[:part_count]
    residual, gain, weight, keep, send = refs[part_count:]
    row_count, width = residual.shape
    vocab = weight.shape[1]
    half = row_count // 2
    hidden = residual[...].astype(f32)
    for part in parts:
        hidden = hidden + part[...].astype(f32)
    scale = lax.rsqrt(jnp.mean(hidden * hidden, axis=1, keepdims=True) + 1e-05)
    normed = (hidden * scale * gain[...]).astype(bf16)
    logits = jnp.dot(normed, weight[...], preferred_element_type=f32)
    row = lax.broadcasted_iota(jnp.int32, (row_count, 1), 0)
    wanted = jnp.zeros((row_count, 1), jnp.int32)
    for r in range(row_count):
        wanted = jnp.where(row == r, targets[r], wanted)
    wanted = wanted - lax.axis_index("tensor") * vocab
    entry = lax.broadcasted_iota(jnp.int32, (row_count, vocab), 1)
    pick = jnp.sum(jnp.where(entry == wanted, logits, 0.0), axis=1, keepdims=True)
    top = jnp.max(logits, axis=1, keepdims=True)
    mass = jnp.sum(jnp.exp(logits - top), axis=1, keepdims=True)
    lane = lax.broadcasted_iota(jnp.int32, (row_count, STAT_LANES), 1)
    stats = jnp.where(lane == 0, top, jnp.where(lane == 1, mass, pick))
    second = lax.axis_index("member") == 1
    for lanes, block in ((slice(0, vocab), logits), (slice(vocab, vocab + STAT_LANES), stats)):
        keep[:, lanes] = jnp.where(second, block[half:], block[:half])
        send[:, lanes] = jnp.where(second, block[:half], block[half:])


def head_rows(targets, parts, residual, gain, weight):
    row_count, width = residual.shape
    vocab = weight.shape[1]
    vmem = pl.BlockSpec(memory_space=pltpu.VMEM)
    shape = jax.ShapeDtypeStruct((row_count // 2, vocab + STAT_LANES), f32)
    return pl.pallas_call(
        functools.partial(head_kernel, len(parts)),
        out_shape=(shape, shape),
        in_specs=[pl.BlockSpec(memory_space=pltpu.SMEM)] + [vmem] * (len(parts) + 3),
        out_specs=(vmem, vmem),
        compiler_params=pltpu.CompilerParams(vmem_limit_bytes=16 << 20),
        name="head_rows",
    )(targets, *parts, residual, gain, weight)


def finish_kernel(tile_count, keep, other, *refs):
    tiles = [ref[...] for ref in refs[:tile_count]]
    mean_out, target_out = refs[tile_count:]
    half, vocab = mean_out.shape
    top = functools.reduce(jnp.maximum, [tile[:, 0:1] for tile in tiles])
    mass = sum(tile[:, 1:2] * jnp.exp(tile[:, 0:1] - top) for tile in tiles)
    pick = sum(tile[:, 2:3] for tile in tiles)
    log_total = top + jnp.log(mass)
    both = log_total[:half] + log_total[half:]
    mean_out[...] = 0.5 * ((keep[:, :vocab] + other[:, :vocab]) - both)
    target = 0.5 * ((pick[:half] + pick[half:]) - both)
    for r in range(half):
        target_out[r] = target[r, 0]


def finish(keep, other, tiles):
    half = keep.shape[0]
    vocab = keep.shape[1] - STAT_LANES
    vmem = pl.BlockSpec(memory_space=pltpu.VMEM)
    return pl.pallas_call(
        functools.partial(finish_kernel, len(tiles)),
        out_shape=(jax.ShapeDtypeStruct((half, vocab), f32), jax.ShapeDtypeStruct((half,), f32)),
        in_specs=[vmem] * (2 + len(tiles)),
        out_specs=(vmem, pl.BlockSpec(memory_space=pltpu.SMEM)),
        compiler_params=pltpu.CompilerParams(vmem_limit_bytes=4 << 20),
        name="finish",
    )(keep, other, *tiles)


def attend_shared(queries, keys, values, lengths, group_size, heads_dev):
    my_rank = lax.axis_index("tensor")
    heads_kv = HEADS // KV_HEADS
    row_count, key_span, head_depth = keys.shape
    kv_index = my_rank // group_size
    slot_first = my_rank % group_size * key_span
    group_query = lax.dynamic_slice_in_dim(queries, kv_index * heads_kv, heads_kv, 1)
    scores = jnp.einsum("rqd,rcd->rqc", group_query, keys, preferred_element_type=jnp.float32)
    scores = scores * (1.0 / head_depth**0.5)
    slot_ids = slot_first + jnp.arange(key_span, dtype=jnp.int32)
    live = (slot_ids[None, :] < lengths[:, None])[:, None, :]
    scores = jnp.where(live, scores, jnp.float32(-1e30))
    top_score = jnp.max(scores, axis=-1)
    weights = jnp.where(live, jnp.exp(scores - top_score[..., None]), jnp.float32(0.0))
    weight_total = jnp.sum(weights, axis=-1)
    weighted = jnp.einsum(
        "rqc,rcd->rqd", weights.astype(jnp.bfloat16), values, preferred_element_type=jnp.float32
    )
    state = (top_score, weight_total, weighted)
    for level in range(group_size.bit_length() - 1):
        partner = swapped(
            (for_sending(state[0]), for_sending(state[1]), for_sending(state[2])), "tensor", level
        )
        state = join_partial(state, partner)
    top_score, weight_total, weighted = state
    head_first = my_rank % group_size * heads_dev
    own_total = lax.dynamic_slice_in_dim(weight_total, head_first, heads_dev, 1)
    own_weighted = lax.dynamic_slice_in_dim(weighted, head_first, heads_dev, 1)
    return (
        (own_weighted / own_total[..., None])
        .reshape(row_count, heads_dev * head_depth)
        .astype(jnp.bfloat16)
    )


def local(queries, keys, values, lengths, targets, residual, out_weight, norm_gain, head_weight):
    axis_width = lax.axis_size("tensor")
    group_size = axis_width // KV_HEADS
    heads_dev = HEADS // axis_width
    direct = axis_width <= 4
    if group_size == 1:
        projected = attend_project(lengths, queries[0], keys[0], values[0], out_weight[0])
    else:
        attended = attend_shared(queries[0], keys[0], values[0], lengths, group_size, heads_dev)
        projected = jnp.dot(attended, out_weight[0], preferred_element_type=jnp.float32).astype(bf16)
    if direct:
        parts = [projected] + [crossed(projected, "tensor", mask) for mask in range(1, axis_width)]
    else:
        parts = [lax.psum(projected, "tensor")]
    head_local = fetch(projected, head_weight[0]) if direct else head_weight[0]
    keep, send = head_rows(targets, parts, residual[0], norm_gain, head_local)
    other = swapped(send, "member", 0)
    vocab = head_weight.shape[2]
    tile = jnp.concatenate([keep[:, vocab:], other[:, vocab:]], axis=0)
    if direct:
        tiles = [tile] + [crossed(tile, "tensor", mask) for mask in range(1, axis_width)]
    else:
        gathered = lax.all_gather(tile, "tensor")
        tiles = [gathered[i] for i in range(axis_width)]
    return finish(keep, other, tiles)


def solution(mesh):
    placed = (
        P("member", "rep", None, None),
        P("member", "rep", "tensor", None),
        P("member", "rep", "tensor", None),
        P("rep"),
        P("rep"),
        P("member", "rep", None),
        P("member", "tensor", None),
        P("member", None),
        P("member", None, "tensor"),
    )
    return jax.shard_map(
        local,
        mesh=mesh,
        in_specs=placed,
        out_specs=(P(("rep", "member"), "tensor"), P(("rep", "member"))),
        check_vma=False,
    )
```

```python
import functools

import jax
import jax.numpy as jnp
from jax import lax
from jax.experimental import pallas as pl
from jax.experimental.pallas import tpu as pltpu
from jax.sharding import PartitionSpec as P

HEADS = 32
KV_HEADS = 4
SLOT_BLOCK = 128
LEAST_LIVE = 256
STAT_LANES = 128
f32 = jnp.float32
bf16 = jnp.bfloat16


def for_sending(shard):

    def short(part):
        return part.astype(jnp.bfloat16) if part.dtype == jnp.float32 else part

    return jax.tree.map(short, shard)


def swapped(block, axis, distance):
    count = lax.axis_size(axis)
    route = []
    for low in range(count):
        high = low | 1 << distance
        if high != low and high < count:
            route += [(low, high), (high, low)]
    return lax.ppermute(block, axis, route)


def crossed(block, axis, mask):
    count = lax.axis_size(axis)
    return lax.ppermute(block, axis, [(i, i ^ mask) for i in range(count)])


def join_partial(earlier, later):
    peak_one, total_one, weighted_one = earlier
    peak_two, total_two, weighted_two = later
    peak_new = jnp.maximum(peak_one, peak_two)
    scale_one = jnp.exp(peak_one - peak_new)
    scale_two = jnp.exp(peak_two - peak_new)
    total_new = total_one * scale_one + total_two * scale_two
    weighted_new = weighted_one * scale_one[..., None] + weighted_two * scale_two[..., None]
    return (peak_new, total_new, weighted_new)


def attend_project_kernel(
    lengths_hbm, queries_hbm, keys_hbm, values_hbm, weight_hbm, out,
    lengths, queries, keys, values, weight, query, scores, probs, heads_out,
    small_sem, key_sem, value_sem, weight_sem,
):
    row_count, span, depth = keys_hbm.shape
    heads_kv = HEADS // KV_HEADS
    pieces = weight_sem.shape[0]
    piece = weight_hbm.shape[0] // pieces
    group_count = 4
    per_group = row_count // group_count
    groups = [range(g * per_group, (g + 1) * per_group) for g in range(group_count)]

    def first_copy(source, target, sem):
        slots = pl.ds(0, LEAST_LIVE)
        return pltpu.make_async_copy(source.at[:, slots], target.at[:, slots], sem)

    def live_copy(source, target, sem, r):
        live = (lengths[r] + (SLOT_BLOCK - 1)) // SLOT_BLOCK * SLOT_BLOCK
        rest = jnp.maximum(live - LEAST_LIVE, SLOT_BLOCK)
        slots = pl.ds(LEAST_LIVE, pl.multiple_of(rest, SLOT_BLOCK))
        return pltpu.make_async_copy(source.at[r, slots], target.at[r, slots], sem.at[r])

    def key_copy(r):
        return live_copy(keys_hbm, keys, key_sem, r)

    def value_copy(r):
        return live_copy(values_hbm, values, value_sem, r)

    def weight_copy(n):
        rows = pl.ds(n * piece, piece)
        return pltpu.make_async_copy(weight_hbm.at[rows], weight.at[rows], weight_sem.at[n])

    lengths_copy = pltpu.make_async_copy(lengths_hbm, lengths, small_sem.at[0])
    queries_copy = pltpu.make_async_copy(queries_hbm, queries, small_sem.at[1])
    first_keys = first_copy(keys_hbm, keys, small_sem.at[2])
    first_values = first_copy(values_hbm, values, small_sem.at[3])
    lengths_copy.start()
    queries_copy.start()
    first_keys.start()
    first_values.start()
    values[:, LEAST_LIVE:] = jnp.zeros((row_count, span - LEAST_LIVE, depth), bf16)
    lengths_copy.wait()
    for r in range(row_count):
        key_copy(r).start()
    for r in range(row_count):
        value_copy(r).start()
    queries_copy.wait()
    query[...] = queries[...].astype(f32)
    first_head = pl.multiple_of(lax.axis_index("tensor") * heads_kv, heads_kv)
    first_keys.wait()
    for g, rows in enumerate(groups):
        for r in rows:
            key_copy(r).wait()
        for n in range(g * pieces // group_count, (g + 1) * pieces // group_count):
            weight_copy(n).start()
        for r in rows:
            own = query[r, pl.ds(first_head, heads_kv), :].astype(bf16)
            score = lax.dot_general(own, keys[r], (((1,), (1,)), ((), ())), preferred_element_type=f32)
            slot = lax.broadcasted_iota(jnp.int32, score.shape, 1)
            scores[r * heads_kv : (r + 1) * heads_kv] = jnp.where(slot < lengths[r], score, -1e30)
    totals = []
    for r in range(row_count):
        score = scores[r * heads_kv : (r + 1) * heads_kv]
        top = jnp.max(score, axis=1, keepdims=True)
        mass = jnp.exp((score - top) * (1.0 / depth**0.5))
        totals.append(jnp.sum(mass, axis=1, keepdims=True))
        probs[r] = mass.astype(bf16)
    first_values.wait()
    for rows in groups:
        for r in rows:
            value_copy(r).wait()
        for r in rows:
            mixed = jnp.dot(probs[r], values[r], preferred_element_type=f32)
            heads_out[r * heads_kv : (r + 1) * heads_kv] = mixed / totals[r]
    attended = jnp.concatenate(
        [heads_out[pl.ds(h, row_count, stride=heads_kv), :] for h in range(heads_kv)], axis=1
    ).astype(bf16)
    total = None
    for n in range(pieces):
        weight_copy(n).wait()
        rows = slice(n * piece, (n + 1) * piece)
        term = jnp.dot(attended[:, rows], weight[rows], preferred_element_type=f32)
        total = term if total is None else total + term
    out[...] = total.astype(out.dtype)


def in_hbm(array):
    return pltpu.with_memory_space_constraint(array, pltpu.HBM)


def attend_project(lengths, queries, keys, values, weight):
    row_count, span, depth = keys.shape
    heads_kv = HEADS // KV_HEADS
    pieces = 8
    return pl.pallas_call(
        attend_project_kernel,
        out_shape=pltpu.VMEM((row_count, weight.shape[1]), bf16),
        in_specs=[pl.BlockSpec(memory_space=pl.ANY)] * 5,
        out_specs=pl.BlockSpec(memory_space=pltpu.VMEM),
        scratch_shapes=[
            pltpu.SMEM(lengths.shape, jnp.int32),
            pltpu.VMEM(queries.shape, bf16),
            pltpu.VMEM(keys.shape, bf16),
            pltpu.VMEM(values.shape, bf16),
            pltpu.VMEM(weight.shape, bf16),
            pltpu.VMEM(queries.shape, f32),
            pltpu.VMEM((row_count * heads_kv, span), f32),
            pltpu.VMEM((row_count, heads_kv, span), bf16),
            pltpu.VMEM((row_count * heads_kv, depth), f32),
            pltpu.SemaphoreType.DMA((4,)),
            pltpu.SemaphoreType.DMA((row_count,)),
            pltpu.SemaphoreType.DMA((row_count,)),
            pltpu.SemaphoreType.DMA((pieces,)),
        ],
        compiler_params=pltpu.CompilerParams(vmem_limit_bytes=57 << 20),
        name="attend_project",
    )(in_hbm(lengths), in_hbm(queries), in_hbm(keys), in_hbm(values), in_hbm(weight))


def relay_kernel(source, one, two, target):
    target[...] = source[...]


def relay(source, one, two):
    vmem = pl.BlockSpec(memory_space=pltpu.VMEM)
    return pl.pallas_call(
        relay_kernel,
        out_shape=pltpu.VMEM(source.shape, source.dtype),
        in_specs=[vmem, pl.BlockSpec(memory_space=pl.ANY), pl.BlockSpec(memory_space=pl.ANY)],
        out_specs=vmem,
        compiler_params=pltpu.CompilerParams(vmem_limit_bytes=1 << 20),
        name="relay",
    )(source, in_hbm(one), in_hbm(two))


def head_kernel(part_count, targets, *refs):
    parts = refs[:part_count]
    residual, gain, weight, keep, send = refs[part_count:]
    row_count, width = residual.shape
    vocab = weight.shape[1]
    half = row_count // 2
    chunks = 4
    chunk = width // chunks
    square = 0.0
    logits = 0.0
    for n in range(chunks):
        columns = slice(n * chunk, (n + 1) * chunk)
        hidden = residual[:, columns].astype(f32)
        for part in parts:
            hidden = hidden + part[:, columns].astype(f32)
        square = square + jnp.sum(hidden * hidden, axis=1, keepdims=True)
        gained = (hidden * gain[:, columns]).astype(bf16)
        logits = logits + jnp.dot(gained, weight[columns], preferred_element_type=f32)
    logits = logits * lax.rsqrt(square / width + 1e-05)
    row = lax.broadcasted_iota(jnp.int32, (row_count, row_count), 0)
    column = lax.broadcasted_iota(jnp.int32, (row_count, row_count), 1)
    wanted = jnp.sum(jnp.where(row == column, targets[...], 0), axis=1, keepdims=True)
    wanted = wanted - lax.axis_index("tensor") * vocab
    entry = lax.broadcasted_iota(jnp.int32, (row_count, vocab), 1)
    pick = jnp.sum(jnp.where(entry == wanted, logits, 0.0), axis=1, keepdims=True)
    top = jnp.max(logits, axis=1, keepdims=True)
    mass = jnp.sum(jnp.exp(logits - top), axis=1, keepdims=True)
    lane = lax.broadcasted_iota(jnp.int32, (row_count, STAT_LANES), 1)
    stats = jnp.where(lane == 0, top, jnp.where(lane == 1, mass, pick))
    second = lax.axis_index("member") == 1
    for lanes, block in ((slice(0, vocab), logits), (slice(vocab, vocab + STAT_LANES), stats)):
        keep[:, lanes] = jnp.where(second, block[half:], block[:half])
        send[:, lanes] = jnp.where(second, block[:half], block[half:])


def head_rows(targets, parts, residual, gain, weight):
    row_count, width = residual.shape
    vocab = weight.shape[1]
    vmem = pl.BlockSpec(memory_space=pltpu.VMEM)
    shape = jax.ShapeDtypeStruct((row_count // 2, vocab + STAT_LANES), f32)
    return pl.pallas_call(
        functools.partial(head_kernel, len(parts)),
        out_shape=(shape, shape),
        in_specs=[vmem] * (len(parts) + 4),
        out_specs=(vmem, vmem),
        compiler_params=pltpu.CompilerParams(vmem_limit_bytes=16 << 20),
        name="head_rows",
    )(targets[None, :], *parts, residual, gain, weight)


def finish_kernel(tile_count, keep, other, *refs):
    tiles = [ref[...] for ref in refs[:tile_count]]
    mean_out, target_out = refs[tile_count:]
    half, vocab = mean_out.shape
    top = functools.reduce(jnp.maximum, [tile[:, 0:1] for tile in tiles])
    mass = sum(tile[:, 1:2] * jnp.exp(tile[:, 0:1] - top) for tile in tiles)
    pick = sum(tile[:, 2:3] for tile in tiles)
    log_total = top + jnp.log(mass)
    both = log_total[:half] + log_total[half:]
    mean_out[...] = 0.5 * ((keep[:, :vocab] + other[:, :vocab]) - both)
    target = 0.5 * ((pick[:half] + pick[half:]) - both)
    row = lax.broadcasted_iota(jnp.int32, (half, half), 0)
    column = lax.broadcasted_iota(jnp.int32, (half, half), 1)
    target_out[...] = jnp.sum(jnp.where(row == column, target, 0.0), axis=0)


def finish(keep, other, tiles):
    half = keep.shape[0]
    vocab = keep.shape[1] - STAT_LANES
    vmem = pl.BlockSpec(memory_space=pltpu.VMEM)
    return pl.pallas_call(
        functools.partial(finish_kernel, len(tiles)),
        out_shape=(jax.ShapeDtypeStruct((half, vocab), f32), jax.ShapeDtypeStruct((half,), f32)),
        in_specs=[vmem] * (2 + len(tiles)),
        out_specs=(vmem, vmem),
        compiler_params=pltpu.CompilerParams(vmem_limit_bytes=4 << 20),
        name="finish",
    )(keep, other, *tiles)


def attend_shared(queries, keys, values, lengths, group_size, heads_dev):
    my_rank = lax.axis_index("tensor")
    heads_kv = HEADS // KV_HEADS
    row_count, key_span, head_depth = keys.shape
    kv_index = my_rank // group_size
    slot_first = my_rank % group_size * key_span
    group_query = lax.dynamic_slice_in_dim(queries, kv_index * heads_kv, heads_kv, 1)
    scores = jnp.einsum("rqd,rcd->rqc", group_query, keys, preferred_element_type=jnp.float32)
    scores = scores * (1.0 / head_depth**0.5)
    slot_ids = slot_first + jnp.arange(key_span, dtype=jnp.int32)
    live = (slot_ids[None, :] < lengths[:, None])[:, None, :]
    scores = jnp.where(live, scores, jnp.float32(-1e30))
    top_score = jnp.max(scores, axis=-1)
    weights = jnp.where(live, jnp.exp(scores - top_score[..., None]), jnp.float32(0.0))
    weight_total = jnp.sum(weights, axis=-1)
    weighted = jnp.einsum(
        "rqc,rcd->rqd", weights.astype(jnp.bfloat16), values, preferred_element_type=jnp.float32
    )
    state = (top_score, weight_total, weighted)
    for level in range(group_size.bit_length() - 1):
        partner = swapped(
            (for_sending(state[0]), for_sending(state[1]), for_sending(state[2])), "tensor", level
        )
        state = join_partial(state, partner)
    top_score, weight_total, weighted = state
    head_first = my_rank % group_size * heads_dev
    own_total = lax.dynamic_slice_in_dim(weight_total, head_first, heads_dev, 1)
    own_weighted = lax.dynamic_slice_in_dim(weighted, head_first, heads_dev, 1)
    return (
        (own_weighted / own_total[..., None])
        .reshape(row_count, heads_dev * head_depth)
        .astype(jnp.bfloat16)
    )


def local(queries, keys, values, lengths, targets, residual, out_weight, norm_gain, head_weight):
    axis_width = lax.axis_size("tensor")
    group_size = axis_width // KV_HEADS
    heads_dev = HEADS // axis_width
    direct = axis_width <= 4
    if group_size == 1:
        projected = attend_project(lengths, queries[0], keys[0], values[0], out_weight[0])
    else:
        attended = attend_shared(queries[0], keys[0], values[0], lengths, group_size, heads_dev)
        projected = jnp.dot(attended, out_weight[0], preferred_element_type=jnp.float32).astype(bf16)
    if direct:
        again = relay(projected, keys[0], values[0])
        parts = [again] + [crossed(again, "tensor", mask) for mask in range(1, axis_width)]
    else:
        parts = [lax.psum(projected, "tensor")]
    head_local = head_weight[0]
    keep, send = head_rows(targets, parts, residual[0], norm_gain, head_local)
    other = swapped(send, "member", 0)
    vocab = head_weight.shape[2]
    tile = jnp.concatenate([keep[:, vocab:], other[:, vocab:]], axis=0)
    if direct:
        tiles = [tile] + [crossed(tile, "tensor", mask) for mask in range(1, axis_width)]
    else:
        gathered = lax.all_gather(tile, "tensor")
        tiles = [gathered[i] for i in range(axis_width)]
    return finish(keep, other, tiles)


def solution(mesh):
    placed = (
        P("member", "rep", None, None),
        P("member", "rep", "tensor", None),
        P("member", "rep", "tensor", None),
        P("rep"),
        P("rep"),
        P("member", "rep", None),
        P("member", "tensor", None),
        P("member", None),
        P("member", None, "tensor"),
    )
    return jax.shard_map(
        local,
        mesh=mesh,
        in_specs=placed,
        out_specs=(P(("rep", "member"), "tensor"), P(("rep", "member"))),
        check_vma=False,
    )
```

```python
import functools

import jax
import jax.numpy as jnp
from jax import lax
from jax.experimental import pallas as pl
from jax.experimental.pallas import tpu as pltpu
from jax.sharding import PartitionSpec as P

HEADS = 32
KV_HEADS = 4
SLOT_BLOCK = 128
LEAST_LIVE = 256
STAT_LANES = 128
f32 = jnp.float32
bf16 = jnp.bfloat16


def for_sending(shard):

    def short(part):
        return part.astype(jnp.bfloat16) if part.dtype == jnp.float32 else part

    return jax.tree.map(short, shard)


def swapped(block, axis, distance):
    count = lax.axis_size(axis)
    route = []
    for low in range(count):
        high = low | 1 << distance
        if high != low and high < count:
            route += [(low, high), (high, low)]
    return lax.ppermute(block, axis, route)


def crossed(block, axis, mask):
    count = lax.axis_size(axis)
    return lax.ppermute(block, axis, [(i, i ^ mask) for i in range(count)])


def join_partial(earlier, later):
    peak_one, total_one, weighted_one = earlier
    peak_two, total_two, weighted_two = later
    peak_new = jnp.maximum(peak_one, peak_two)
    scale_one = jnp.exp(peak_one - peak_new)
    scale_two = jnp.exp(peak_two - peak_new)
    total_new = total_one * scale_one + total_two * scale_two
    weighted_new = weighted_one * scale_one[..., None] + weighted_two * scale_two[..., None]
    return (peak_new, total_new, weighted_new)


def attend_project_kernel(
    lengths_hbm, queries_hbm, keys_hbm, values_hbm, weight_hbm, out,
    lengths, queries, keys, values, weight, query, scores, probs, heads_out,
    small_sem, key_sem, value_sem, weight_sem,
):
    row_count, span, depth = keys_hbm.shape
    heads_kv = HEADS // KV_HEADS
    pieces = weight_sem.shape[0]
    piece = weight_hbm.shape[0] // pieces
    group_count = 4
    per_group = row_count // group_count
    groups = [range(g * per_group, (g + 1) * per_group) for g in range(group_count)]

    def first_copy(source, target, sem):
        slots = pl.ds(0, LEAST_LIVE)
        return pltpu.make_async_copy(source.at[:, slots], target.at[:, slots], sem)

    def live_copy(source, target, sem, r):
        live = (lengths[r] + (SLOT_BLOCK - 1)) // SLOT_BLOCK * SLOT_BLOCK
        rest = jnp.maximum(live - LEAST_LIVE, SLOT_BLOCK)
        slots = pl.ds(LEAST_LIVE, pl.multiple_of(rest, SLOT_BLOCK))
        return pltpu.make_async_copy(source.at[r, slots], target.at[r, slots], sem.at[r])

    def key_copy(r):
        return live_copy(keys_hbm, keys, key_sem, r)

    def value_copy(r):
        return live_copy(values_hbm, values, value_sem, r)

    def weight_copy(n):
        rows = pl.ds(n * piece, piece)
        return pltpu.make_async_copy(weight_hbm.at[rows], weight.at[rows], weight_sem.at[n])

    lengths_copy = pltpu.make_async_copy(lengths_hbm, lengths, small_sem.at[0])
    queries_copy = pltpu.make_async_copy(queries_hbm, queries, small_sem.at[1])
    first_keys = first_copy(keys_hbm, keys, small_sem.at[2])
    first_values = first_copy(values_hbm, values, small_sem.at[3])
    lengths_copy.start()
    queries_copy.start()
    first_keys.start()
    first_values.start()
    values[:, LEAST_LIVE:] = jnp.zeros((row_count, span - LEAST_LIVE, depth), bf16)
    lengths_copy.wait()
    for r in range(row_count):
        key_copy(r).start()
    for r in range(row_count):
        value_copy(r).start()
    queries_copy.wait()
    query[...] = queries[...].astype(f32)
    first_head = pl.multiple_of(lax.axis_index("tensor") * heads_kv, heads_kv)
    first_keys.wait()
    for g, rows in enumerate(groups):
        for r in rows:
            key_copy(r).wait()
        for n in range(g * pieces // group_count, (g + 1) * pieces // group_count):
            weight_copy(n).start()
        for r in rows:
            own = query[r, pl.ds(first_head, heads_kv), :].astype(bf16)
            score = lax.dot_general(own, keys[r], (((1,), (1,)), ((), ())), preferred_element_type=f32)
            slot = lax.broadcasted_iota(jnp.int32, score.shape, 1)
            scores[r * heads_kv : (r + 1) * heads_kv] = jnp.where(slot < lengths[r], score, -1e30)
    totals = []
    for r in range(row_count):
        score = scores[r * heads_kv : (r + 1) * heads_kv]
        top = jnp.max(score, axis=1, keepdims=True)
        mass = jnp.exp((score - top) * (1.0 / depth**0.5))
        totals.append(jnp.sum(mass, axis=1, keepdims=True))
        probs[r] = mass.astype(bf16)
    first_values.wait()
    for rows in groups:
        for r in rows:
            value_copy(r).wait()
        for r in rows:
            mixed = jnp.dot(probs[r], values[r], preferred_element_type=f32)
            heads_out[r * heads_kv : (r + 1) * heads_kv] = mixed / totals[r]
    attended = jnp.concatenate(
        [heads_out[pl.ds(h, row_count, stride=heads_kv), :] for h in range(heads_kv)], axis=1
    ).astype(bf16)
    total = None
    for n in range(pieces):
        weight_copy(n).wait()
        rows = slice(n * piece, (n + 1) * piece)
        term = jnp.dot(attended[:, rows], weight[rows], preferred_element_type=f32)
        total = term if total is None else total + term
    out[...] = total.astype(out.dtype)


def in_hbm(array):
    return pltpu.with_memory_space_constraint(array, pltpu.HBM)


def attend_project(lengths, queries, keys, values, weight):
    row_count, span, depth = keys.shape
    heads_kv = HEADS // KV_HEADS
    pieces = 8
    return pl.pallas_call(
        attend_project_kernel,
        out_shape=pltpu.VMEM((row_count, weight.shape[1]), bf16),
        in_specs=[pl.BlockSpec(memory_space=pl.ANY)] * 5,
        out_specs=pl.BlockSpec(memory_space=pltpu.VMEM),
        scratch_shapes=[
            pltpu.SMEM(lengths.shape, jnp.int32),
            pltpu.VMEM(queries.shape, bf16),
            pltpu.VMEM(keys.shape, bf16),
            pltpu.VMEM(values.shape, bf16),
            pltpu.VMEM(weight.shape, bf16),
            pltpu.VMEM(queries.shape, f32),
            pltpu.VMEM((row_count * heads_kv, span), f32),
            pltpu.VMEM((row_count, heads_kv, span), bf16),
            pltpu.VMEM((row_count * heads_kv, depth), f32),
            pltpu.SemaphoreType.DMA((4,)),
            pltpu.SemaphoreType.DMA((row_count,)),
            pltpu.SemaphoreType.DMA((row_count,)),
            pltpu.SemaphoreType.DMA((pieces,)),
        ],
        compiler_params=pltpu.CompilerParams(vmem_limit_bytes=57 << 20),
        name="attend_project",
    )(in_hbm(lengths), in_hbm(queries), in_hbm(keys), in_hbm(values), in_hbm(weight))


def relay_kernel(source, one, two, target):
    target[...] = source[...]


def relay(source, one, two):
    vmem = pl.BlockSpec(memory_space=pltpu.VMEM)
    return pl.pallas_call(
        relay_kernel,
        out_shape=pltpu.VMEM(source.shape, source.dtype),
        in_specs=[vmem, pl.BlockSpec(memory_space=pl.ANY), pl.BlockSpec(memory_space=pl.ANY)],
        out_specs=vmem,
        compiler_params=pltpu.CompilerParams(vmem_limit_bytes=1 << 20),
        name="relay",
    )(source, in_hbm(one), in_hbm(two))


def head_kernel(part_count, targets, *refs):
    parts = refs[:part_count]
    residual, gain, weight, keep, send, own = refs[part_count:]
    row_count, width = residual.shape
    vocab = weight.shape[1]
    half = row_count // 2
    chunks = 4
    chunk = width // chunks
    square = 0.0
    logits = 0.0
    for n in range(chunks):
        columns = slice(n * chunk, (n + 1) * chunk)
        hidden = residual[:, columns].astype(f32)
        for part in parts:
            hidden = hidden + part[:, columns].astype(f32)
        square = square + jnp.sum(hidden * hidden, axis=1, keepdims=True)
        gained = (hidden * gain[:, columns]).astype(bf16)
        logits = logits + jnp.dot(gained, weight[columns], preferred_element_type=f32)
    logits = logits * lax.rsqrt(square / width + 1e-05)
    row = lax.broadcasted_iota(jnp.int32, (row_count, row_count), 0)
    column = lax.broadcasted_iota(jnp.int32, (row_count, row_count), 1)
    wanted = jnp.sum(jnp.where(row == column, targets[...], 0), axis=1, keepdims=True)
    wanted = wanted - lax.axis_index("tensor") * vocab
    entry = lax.broadcasted_iota(jnp.int32, (row_count, vocab), 1)
    pick = jnp.sum(jnp.where(entry == wanted, logits, 0.0), axis=1, keepdims=True)
    top = jnp.max(logits, axis=1, keepdims=True)
    mass = jnp.sum(jnp.exp(logits - top), axis=1, keepdims=True)
    lane = lax.broadcasted_iota(jnp.int32, (row_count, STAT_LANES), 1)
    stats = jnp.where(lane == 0, top, jnp.where(lane == 1, mass, pick))
    own[...] = stats
    second = lax.axis_index("member") == 1
    for lanes, block in ((slice(0, vocab), logits), (slice(vocab, vocab + STAT_LANES), stats)):
        keep[:, lanes] = jnp.where(second, block[half:], block[:half])
        send[:, lanes] = jnp.where(second, block[:half], block[half:])


def head_rows(targets, parts, residual, gain, weight):
    row_count, width = residual.shape
    vocab = weight.shape[1]
    vmem = pl.BlockSpec(memory_space=pltpu.VMEM)
    shape = jax.ShapeDtypeStruct((row_count // 2, vocab + STAT_LANES), f32)
    return pl.pallas_call(
        functools.partial(head_kernel, len(parts)),
        out_shape=(shape, shape, jax.ShapeDtypeStruct((row_count, STAT_LANES), f32)),
        in_specs=[vmem] * (len(parts) + 4),
        out_specs=(vmem, vmem, vmem),
        compiler_params=pltpu.CompilerParams(vmem_limit_bytes=16 << 20),
        name="head_rows",
    )(targets[None, :], *parts, residual, gain, weight)


def finish_kernel(tile_count, across, keep, other, *refs):
    tiles = [ref[...] for ref in refs[:tile_count]]
    mean_out, target_out = refs[-2:]
    half, vocab = mean_out.shape
    if across:
        ours, theirs = (ref[...] for ref in refs[tile_count:-2])
        second = lax.axis_index("member") == 1
        mine = [jnp.where(second, block[half:], block[:half]) for block in (ours, theirs)]
        tiles.append(jnp.concatenate(mine, axis=0))
    top = functools.reduce(jnp.maximum, [tile[:, 0:1] for tile in tiles])
    mass = sum(tile[:, 1:2] * jnp.exp(tile[:, 0:1] - top) for tile in tiles)
    pick = sum(tile[:, 2:3] for tile in tiles)
    log_total = top + jnp.log(mass)
    both = log_total[:half] + log_total[half:]
    mean_out[...] = 0.5 * ((keep[:, :vocab] + other[:, :vocab]) - both)
    target = 0.5 * ((pick[:half] + pick[half:]) - both)
    row = lax.broadcasted_iota(jnp.int32, (half, half), 0)
    column = lax.broadcasted_iota(jnp.int32, (half, half), 1)
    target_out[...] = jnp.sum(jnp.where(row == column, target, 0.0), axis=0)


def finish(keep, other, tiles, across=()):
    half = keep.shape[0]
    vocab = keep.shape[1] - STAT_LANES
    vmem = pl.BlockSpec(memory_space=pltpu.VMEM)
    return pl.pallas_call(
        functools.partial(finish_kernel, len(tiles), bool(across)),
        out_shape=(jax.ShapeDtypeStruct((half, vocab), f32), jax.ShapeDtypeStruct((half,), f32)),
        in_specs=[vmem] * (2 + len(tiles) + len(across)),
        out_specs=(vmem, vmem),
        compiler_params=pltpu.CompilerParams(vmem_limit_bytes=4 << 20),
        name="finish",
    )(keep, other, *tiles, *across)


def attend_shared(queries, keys, values, lengths, group_size, heads_dev):
    my_rank = lax.axis_index("tensor")
    heads_kv = HEADS // KV_HEADS
    row_count, key_span, head_depth = keys.shape
    kv_index = my_rank // group_size
    slot_first = my_rank % group_size * key_span
    group_query = lax.dynamic_slice_in_dim(queries, kv_index * heads_kv, heads_kv, 1)
    scores = jnp.einsum("rqd,rcd->rqc", group_query, keys, preferred_element_type=jnp.float32)
    scores = scores * (1.0 / head_depth**0.5)
    slot_ids = slot_first + jnp.arange(key_span, dtype=jnp.int32)
    live = (slot_ids[None, :] < lengths[:, None])[:, None, :]
    scores = jnp.where(live, scores, jnp.float32(-1e30))
    top_score = jnp.max(scores, axis=-1)
    weights = jnp.where(live, jnp.exp(scores - top_score[..., None]), jnp.float32(0.0))
    weight_total = jnp.sum(weights, axis=-1)
    weighted = jnp.einsum(
        "rqc,rcd->rqd", weights.astype(jnp.bfloat16), values, preferred_element_type=jnp.float32
    )
    state = (top_score, weight_total, weighted)
    for level in range(group_size.bit_length() - 1):
        partner = swapped(
            (for_sending(state[0]), for_sending(state[1]), for_sending(state[2])), "tensor", level
        )
        state = join_partial(state, partner)
    top_score, weight_total, weighted = state
    head_first = my_rank % group_size * heads_dev
    own_total = lax.dynamic_slice_in_dim(weight_total, head_first, heads_dev, 1)
    own_weighted = lax.dynamic_slice_in_dim(weighted, head_first, heads_dev, 1)
    return (
        (own_weighted / own_total[..., None])
        .reshape(row_count, heads_dev * head_depth)
        .astype(jnp.bfloat16)
    )


def local(queries, keys, values, lengths, targets, residual, out_weight, norm_gain, head_weight):
    axis_width = lax.axis_size("tensor")
    group_size = axis_width // KV_HEADS
    heads_dev = HEADS // axis_width
    direct = axis_width == 4
    if group_size == 1:
        projected = attend_project(lengths, queries[0], keys[0], values[0], out_weight[0])
    else:
        attended = attend_shared(queries[0], keys[0], values[0], lengths, group_size, heads_dev)
        projected = jnp.dot(attended, out_weight[0], preferred_element_type=jnp.float32).astype(bf16)
    if direct:
        again = relay(projected, keys[0], values[0])
        parts = [again] + [crossed(again, "tensor", mask) for mask in range(1, axis_width)]
    else:
        parts = [lax.psum(projected, "tensor")]
    head_local = head_weight[0]
    keep, send, stats = head_rows(targets, parts, residual[0], norm_gain, head_weight[0])
    other = swapped(send, "member", 0)
    vocab = head_weight.shape[2]
    tile = jnp.concatenate([keep[:, vocab:], other[:, vocab:]], axis=0)
    if direct:
        ours = crossed(stats, "tensor", 3)
        tiles = [tile, crossed(tile, "tensor", 1), crossed(tile, "tensor", 2)]
        held, _ = lax.optimization_barrier((ours, tiles[2]))
        return finish(keep, other, tiles, (ours, swapped(held, "member", 0)))
    gathered = lax.all_gather(tile, "tensor")
    return finish(keep, other, [gathered[i] for i in range(axis_width)])


def solution(mesh):
    placed = (
        P("member", "rep", None, None),
        P("member", "rep", "tensor", None),
        P("member", "rep", "tensor", None),
        P("rep"),
        P("rep"),
        P("member", "rep", None),
        P("member", "tensor", None),
        P("member", None),
        P("member", None, "tensor"),
    )
    return jax.shard_map(
        local,
        mesh=mesh,
        in_specs=placed,
        out_specs=(P(("rep", "member"), "tensor"), P(("rep", "member"))),
        check_vma=False,
    )
```

```python
import functools

import jax
import jax.numpy as jnp
from jax import lax
from jax.experimental import pallas as pl
from jax.experimental.pallas import tpu as pltpu
from jax.sharding import PartitionSpec as P

HEADS = 32
KV_HEADS = 4
SLOT_BLOCK = 128
LEAST_LIVE = 256
STAT_LANES = 128
f32 = jnp.float32
bf16 = jnp.bfloat16


def for_sending(shard):

    def short(part):
        return part.astype(jnp.bfloat16) if part.dtype == jnp.float32 else part

    return jax.tree.map(short, shard)


def swapped(block, axis, distance):
    count = lax.axis_size(axis)
    route = []
    for low in range(count):
        high = low | 1 << distance
        if high != low and high < count:
            route += [(low, high), (high, low)]
    return lax.ppermute(block, axis, route)


def crossed(block, axis, mask):
    count = lax.axis_size(axis)
    return lax.ppermute(block, axis, [(i, i ^ mask) for i in range(count)])


def split_crossed(block, masks):
    count = lax.axis_size("tensor")
    route = [(m * count + i, m * count + (i ^ mask)) for m, mask in enumerate(masks) for i in range(count)]
    return lax.ppermute(block, ("member", "tensor"), route)


def join_partial(earlier, later):
    peak_one, total_one, weighted_one = earlier
    peak_two, total_two, weighted_two = later
    peak_new = jnp.maximum(peak_one, peak_two)
    scale_one = jnp.exp(peak_one - peak_new)
    scale_two = jnp.exp(peak_two - peak_new)
    total_new = total_one * scale_one + total_two * scale_two
    weighted_new = weighted_one * scale_one[..., None] + weighted_two * scale_two[..., None]
    return (peak_new, total_new, weighted_new)


def attend_project_kernel(
    lengths_hbm, queries_hbm, keys_hbm, values_hbm, weight_hbm, out,
    lengths, queries, keys, values, weight, query, scores, probs, heads_out,
    small_sem, key_sem, value_sem, weight_sem,
):
    row_count, span, depth = keys_hbm.shape
    heads_kv = HEADS // KV_HEADS
    pieces = weight_sem.shape[0]
    piece = weight_hbm.shape[0] // pieces
    group_count = 2
    per_group = row_count // group_count
    groups = [range(g * per_group, (g + 1) * per_group) for g in range(group_count)]

    def first_copy(source, target, sem):
        slots = pl.ds(0, LEAST_LIVE)
        return pltpu.make_async_copy(source.at[:, slots], target.at[:, slots], sem)

    def live_copy(source, target, sem, r):
        live = (lengths[r] + (SLOT_BLOCK - 1)) // SLOT_BLOCK * SLOT_BLOCK
        rest = jnp.maximum(live - LEAST_LIVE, SLOT_BLOCK)
        slots = pl.ds(LEAST_LIVE, pl.multiple_of(rest, SLOT_BLOCK))
        return pltpu.make_async_copy(source.at[r, slots], target.at[r, slots], sem.at[r])

    def key_copy(r):
        return live_copy(keys_hbm, keys, key_sem, r)

    def value_copy(r):
        return live_copy(values_hbm, values, value_sem, r)

    def weight_copy(n):
        rows = pl.ds(n * piece, piece)
        return pltpu.make_async_copy(weight_hbm.at[rows], weight.at[rows], weight_sem.at[n])

    lengths_copy = pltpu.make_async_copy(lengths_hbm, lengths, small_sem.at[0])
    queries_copy = pltpu.make_async_copy(queries_hbm, queries, small_sem.at[1])
    first_keys = first_copy(keys_hbm, keys, small_sem.at[2])
    first_values = first_copy(values_hbm, values, small_sem.at[3])
    lengths_copy.start()
    queries_copy.start()
    first_keys.start()
    first_values.start()
    values[:, LEAST_LIVE:] = jnp.zeros((row_count, span - LEAST_LIVE, depth), bf16)
    lengths_copy.wait()
    for r in range(row_count):
        key_copy(r).start()
    for r in range(row_count):
        value_copy(r).start()
    queries_copy.wait()
    query[...] = queries[...].astype(f32)
    first_head = pl.multiple_of(lax.axis_index("tensor") * heads_kv, heads_kv)
    first_keys.wait()
    ahead = pieces // 4
    for n in range(ahead):
        weight_copy(n).start()
    for g, rows in enumerate(groups):
        for r in rows:
            key_copy(r).wait()
        share = (pieces - ahead) // group_count
        for n in range(ahead + g * share, ahead + (g + 1) * share):
            weight_copy(n).start()
        for r in rows:
            own = query[r, pl.ds(first_head, heads_kv), :].astype(bf16)
            score = lax.dot_general(own, keys[r], (((1,), (1,)), ((), ())), preferred_element_type=f32)
            slot = lax.broadcasted_iota(jnp.int32, score.shape, 1)
            scores[r * heads_kv : (r + 1) * heads_kv] = jnp.where(slot < lengths[r], score, -1e30)
    totals = []
    for r in range(row_count):
        score = scores[r * heads_kv : (r + 1) * heads_kv]
        top = jnp.max(score, axis=1, keepdims=True)
        mass = jnp.exp((score - top) * (1.0 / depth**0.5))
        totals.append(jnp.sum(mass, axis=1, keepdims=True))
        probs[r] = mass.astype(bf16)
    first_values.wait()
    for rows in groups:
        for r in rows:
            value_copy(r).wait()
        for r in rows:
            mixed = jnp.dot(probs[r], values[r], preferred_element_type=f32)
            heads_out[r * heads_kv : (r + 1) * heads_kv] = mixed / totals[r]
    attended = jnp.concatenate(
        [heads_out[pl.ds(h, row_count, stride=heads_kv), :] for h in range(heads_kv)], axis=1
    ).astype(bf16)
    total = None
    for n in range(pieces):
        weight_copy(n).wait()
        rows = slice(n * piece, (n + 1) * piece)
        term = jnp.dot(attended[:, rows], weight[rows], preferred_element_type=f32)
        total = term if total is None else total + term
    out[...] = total.astype(out.dtype)


def in_hbm(array):
    return pltpu.with_memory_space_constraint(array, pltpu.HBM)


def attend_project(lengths, queries, keys, values, weight):
    row_count, span, depth = keys.shape
    heads_kv = HEADS // KV_HEADS
    pieces = 8
    return pl.pallas_call(
        attend_project_kernel,
        out_shape=pltpu.VMEM((row_count, weight.shape[1]), bf16),
        in_specs=[pl.BlockSpec(memory_space=pl.ANY)] * 5,
        out_specs=pl.BlockSpec(memory_space=pltpu.VMEM),
        scratch_shapes=[
            pltpu.SMEM(lengths.shape, jnp.int32),
            pltpu.VMEM(queries.shape, bf16),
            pltpu.VMEM(keys.shape, bf16),
            pltpu.VMEM(values.shape, bf16),
            pltpu.VMEM(weight.shape, bf16),
            pltpu.VMEM(queries.shape, f32),
            pltpu.VMEM((row_count * heads_kv, span), f32),
            pltpu.VMEM((row_count, heads_kv, span), bf16),
            pltpu.VMEM((row_count * heads_kv, depth), f32),
            pltpu.SemaphoreType.DMA((4,)),
            pltpu.SemaphoreType.DMA((row_count,)),
            pltpu.SemaphoreType.DMA((row_count,)),
            pltpu.SemaphoreType.DMA((pieces,)),
        ],
        compiler_params=pltpu.CompilerParams(vmem_limit_bytes=57 << 20),
        name="attend_project",
    )(in_hbm(lengths), in_hbm(queries), in_hbm(keys), in_hbm(values), in_hbm(weight))


def relay_kernel(source, one, two, target):
    target[...] = source[...]


def relay(source, one, two):
    vmem = pl.BlockSpec(memory_space=pltpu.VMEM)
    return pl.pallas_call(
        relay_kernel,
        out_shape=pltpu.VMEM(source.shape, source.dtype),
        in_specs=[vmem, pl.BlockSpec(memory_space=pl.ANY), pl.BlockSpec(memory_space=pl.ANY)],
        out_specs=vmem,
        compiler_params=pltpu.CompilerParams(vmem_limit_bytes=1 << 20),
        name="relay",
    )(source, in_hbm(one), in_hbm(two))


def head_kernel(part_count, targets, *refs):
    parts = refs[:part_count]
    residual, gain, weight, keep, send, own = refs[part_count:]
    row_count, width = residual.shape
    vocab = weight.shape[1]
    half = row_count // 2
    chunks = 4
    chunk = width // chunks
    square = 0.0
    logits = 0.0
    for n in range(chunks):
        columns = slice(n * chunk, (n + 1) * chunk)
        hidden = residual[:, columns].astype(f32)
        for part in parts:
            hidden = hidden + part[:, columns].astype(f32)
        square = square + jnp.sum(hidden * hidden, axis=1, keepdims=True)
        gained = (hidden * gain[:, columns]).astype(bf16)
        logits = logits + jnp.dot(gained, weight[columns], preferred_element_type=f32)
    logits = logits * lax.rsqrt(square / width + 1e-05)
    row = lax.broadcasted_iota(jnp.int32, (row_count, row_count), 0)
    column = lax.broadcasted_iota(jnp.int32, (row_count, row_count), 1)
    wanted = jnp.sum(jnp.where(row == column, targets[...], 0), axis=1, keepdims=True)
    wanted = wanted - lax.axis_index("tensor") * vocab
    entry = lax.broadcasted_iota(jnp.int32, (row_count, vocab), 1)
    pick = jnp.sum(jnp.where(entry == wanted, logits, 0.0), axis=1, keepdims=True)
    top = jnp.max(logits, axis=1, keepdims=True)
    mass = jnp.sum(jnp.exp(logits - top), axis=1, keepdims=True)
    lane = lax.broadcasted_iota(jnp.int32, (row_count, STAT_LANES), 1)
    stats = jnp.where(lane == 0, top, jnp.where(lane == 1, mass, pick))
    own[...] = stats
    second = lax.axis_index("member") == 1
    for lanes, block in ((slice(0, vocab), logits), (slice(vocab, vocab + STAT_LANES), stats)):
        keep[:, lanes] = jnp.where(second, block[half:], block[:half])
        send[:, lanes] = jnp.where(second, block[:half], block[half:])


def head_rows(targets, parts, residual, gain, weight):
    row_count, width = residual.shape
    vocab = weight.shape[1]
    vmem = pl.BlockSpec(memory_space=pltpu.VMEM)
    shape = jax.ShapeDtypeStruct((row_count // 2, vocab + STAT_LANES), f32)
    return pl.pallas_call(
        functools.partial(head_kernel, len(parts)),
        out_shape=(shape, shape, jax.ShapeDtypeStruct((row_count, STAT_LANES), f32)),
        in_specs=[vmem] * (len(parts) + 4),
        out_specs=(vmem, vmem, vmem),
        compiler_params=pltpu.CompilerParams(vmem_limit_bytes=16 << 20),
        name="head_rows",
    )(targets[None, :], *parts, residual, gain, weight)


def finish_kernel(tile_count, across, keep, other, *refs):
    tiles = [ref[...] for ref in refs[:tile_count]]
    mean_out, target_out = refs[-2:]
    half, vocab = mean_out.shape
    if across:
        ours, theirs = (ref[...] for ref in refs[tile_count:-2])
        second = lax.axis_index("member") == 1
        mine = [jnp.where(second, block[half:], block[:half]) for block in (ours, theirs)]
        tiles.append(jnp.concatenate(mine, axis=0))
    top = functools.reduce(jnp.maximum, [tile[:, 0:1] for tile in tiles])
    mass = sum(tile[:, 1:2] * jnp.exp(tile[:, 0:1] - top) for tile in tiles)
    pick = sum(tile[:, 2:3] for tile in tiles)
    log_total = top + jnp.log(mass)
    both = log_total[:half] + log_total[half:]
    mean_out[...] = 0.5 * ((keep[:, :vocab] + other[:, :vocab]) - both)
    target = 0.5 * ((pick[:half] + pick[half:]) - both)
    row = lax.broadcasted_iota(jnp.int32, (half, half), 0)
    column = lax.broadcasted_iota(jnp.int32, (half, half), 1)
    target_out[...] = jnp.sum(jnp.where(row == column, target, 0.0), axis=0)


def finish(keep, other, tiles, across=()):
    half = keep.shape[0]
    vocab = keep.shape[1] - STAT_LANES
    vmem = pl.BlockSpec(memory_space=pltpu.VMEM)
    return pl.pallas_call(
        functools.partial(finish_kernel, len(tiles), bool(across)),
        out_shape=(jax.ShapeDtypeStruct((half, vocab), f32), jax.ShapeDtypeStruct((half,), f32)),
        in_specs=[vmem] * (2 + len(tiles) + len(across)),
        out_specs=(vmem, vmem),
        compiler_params=pltpu.CompilerParams(vmem_limit_bytes=4 << 20),
        name="finish",
    )(keep, other, *tiles, *across)


def attend_shared(queries, keys, values, lengths, group_size, heads_dev):
    my_rank = lax.axis_index("tensor")
    heads_kv = HEADS // KV_HEADS
    row_count, key_span, head_depth = keys.shape
    kv_index = my_rank // group_size
    slot_first = my_rank % group_size * key_span
    group_query = lax.dynamic_slice_in_dim(queries, kv_index * heads_kv, heads_kv, 1)
    scores = jnp.einsum("rqd,rcd->rqc", group_query, keys, preferred_element_type=jnp.float32)
    scores = scores * (1.0 / head_depth**0.5)
    slot_ids = slot_first + jnp.arange(key_span, dtype=jnp.int32)
    live = (slot_ids[None, :] < lengths[:, None])[:, None, :]
    scores = jnp.where(live, scores, jnp.float32(-1e30))
    top_score = jnp.max(scores, axis=-1)
    weights = jnp.where(live, jnp.exp(scores - top_score[..., None]), jnp.float32(0.0))
    weight_total = jnp.sum(weights, axis=-1)
    weighted = jnp.einsum(
        "rqc,rcd->rqd", weights.astype(jnp.bfloat16), values, preferred_element_type=jnp.float32
    )
    state = (top_score, weight_total, weighted)
    for level in range(group_size.bit_length() - 1):
        partner = swapped(
            (for_sending(state[0]), for_sending(state[1]), for_sending(state[2])), "tensor", level
        )
        state = join_partial(state, partner)
    top_score, weight_total, weighted = state
    head_first = my_rank % group_size * heads_dev
    own_total = lax.dynamic_slice_in_dim(weight_total, head_first, heads_dev, 1)
    own_weighted = lax.dynamic_slice_in_dim(weighted, head_first, heads_dev, 1)
    return (
        (own_weighted / own_total[..., None])
        .reshape(row_count, heads_dev * head_depth)
        .astype(jnp.bfloat16)
    )


def local(queries, keys, values, lengths, targets, residual, out_weight, norm_gain, head_weight):
    axis_width = lax.axis_size("tensor")
    group_size = axis_width // KV_HEADS
    heads_dev = HEADS // axis_width
    direct = axis_width == 4
    if group_size == 1:
        projected = attend_project(lengths, queries[0], keys[0], values[0], out_weight[0])
    else:
        attended = attend_shared(queries[0], keys[0], values[0], lengths, group_size, heads_dev)
        projected = jnp.dot(attended, out_weight[0], preferred_element_type=jnp.float32).astype(bf16)
    if direct:
        again = relay(projected, keys[0], values[0])
        parts = [again, split_crossed(again, (2, 1)), split_crossed(again, (1, 2)), crossed(again, "tensor", 3)]
    else:
        parts = [lax.psum(projected, "tensor")]
    head_local = head_weight[0]
    keep, send, stats = head_rows(targets, parts, residual[0], norm_gain, head_weight[0])
    other = swapped(send, "member", 0)
    vocab = head_weight.shape[2]
    tile = jnp.concatenate([keep[:, vocab:], other[:, vocab:]], axis=0)
    if direct:
        ours = crossed(stats, "tensor", 3)
        tiles = [tile, split_crossed(tile, (2, 1)), split_crossed(tile, (1, 2))]
        held, _ = lax.optimization_barrier((ours, tiles[2]))
        return finish(keep, other, tiles, (ours, swapped(held, "member", 0)))
    gathered = lax.all_gather(tile, "tensor")
    return finish(keep, other, [gathered[i] for i in range(axis_width)])


def solution(mesh):
    placed = (
        P("member", "rep", None, None),
        P("member", "rep", "tensor", None),
        P("member", "rep", "tensor", None),
        P("rep"),
        P("rep"),
        P("member", "rep", None),
        P("member", "tensor", None),
        P("member", None),
        P("member", None, "tensor"),
    )
    return jax.shard_map(
        local,
        mesh=mesh,
        in_specs=placed,
        out_specs=(P(("rep", "member"), "tensor"), P(("rep", "member"))),
        check_vma=False,
    )
```

```python
import functools

import jax
import jax.numpy as jnp
from jax import lax
from jax.experimental import pallas as pl
from jax.experimental.pallas import tpu as pltpu
from jax.sharding import PartitionSpec as P

HEADS = 32
KV_HEADS = 4
SLOT_BLOCK = 128
LEAST_LIVE = 256
LANES = 128
STAT_LANES = 3 * LANES
f32 = jnp.float32
bf16 = jnp.bfloat16


def for_sending(shard):

    def short(part):
        return part.astype(jnp.bfloat16) if part.dtype == jnp.float32 else part

    return jax.tree.map(short, shard)


def swapped(block, axis, distance):
    count = lax.axis_size(axis)
    route = []
    for low in range(count):
        high = low | 1 << distance
        if high != low and high < count:
            route += [(low, high), (high, low)]
    return lax.ppermute(block, axis, route)


def crossed(block, axis, mask):
    count = lax.axis_size(axis)
    return lax.ppermute(block, axis, [(i, i ^ mask) for i in range(count)])


def join_partial(earlier, later):
    peak_one, total_one, weighted_one = earlier
    peak_two, total_two, weighted_two = later
    peak_new = jnp.maximum(peak_one, peak_two)
    scale_one = jnp.exp(peak_one - peak_new)
    scale_two = jnp.exp(peak_two - peak_new)
    total_new = total_one * scale_one + total_two * scale_two
    weighted_new = weighted_one * scale_one[..., None] + weighted_two * scale_two[..., None]
    return (peak_new, total_new, weighted_new)


def attend_project_kernel(
    lengths_hbm, queries_hbm, keys_hbm, values_hbm, weight_hbm, out,
    lengths, queries, keys, values, weight, query, scores, probs, heads_out,
    small_sem, key_sem, value_sem, weight_sem,
):
    row_count, span, depth = keys_hbm.shape
    heads_kv = HEADS // KV_HEADS
    pieces = weight_sem.shape[0]
    piece = weight_hbm.shape[0] // pieces
    group_count = 4
    per_group = row_count // group_count
    groups = [range(g * per_group, (g + 1) * per_group) for g in range(group_count)]

    def first_copy(source, target, sem):
        slots = pl.ds(0, LEAST_LIVE)
        return pltpu.make_async_copy(source.at[:, slots], target.at[:, slots], sem)

    def live_copy(source, target, sem, r):
        live = (lengths[r] + (SLOT_BLOCK - 1)) // SLOT_BLOCK * SLOT_BLOCK
        rest = jnp.maximum(live - LEAST_LIVE, SLOT_BLOCK)
        slots = pl.ds(LEAST_LIVE, pl.multiple_of(rest, SLOT_BLOCK))
        return pltpu.make_async_copy(source.at[r, slots], target.at[r, slots], sem.at[r])

    def key_copy(r):
        return live_copy(keys_hbm, keys, key_sem, r)

    def value_copy(r):
        return live_copy(values_hbm, values, value_sem, r)

    def weight_copy(n):
        rows = pl.ds(n * piece, piece)
        return pltpu.make_async_copy(weight_hbm.at[rows], weight.at[rows], weight_sem.at[n])

    lengths_copy = pltpu.make_async_copy(lengths_hbm, lengths, small_sem.at[0])
    queries_copy = pltpu.make_async_copy(queries_hbm, queries, small_sem.at[1])
    first_keys = first_copy(keys_hbm, keys, small_sem.at[2])
    first_values = first_copy(values_hbm, values, small_sem.at[3])
    lengths_copy.start()
    queries_copy.start()
    first_keys.start()
    first_values.start()
    values[:, LEAST_LIVE:] = jnp.zeros((row_count, span - LEAST_LIVE, depth), bf16)
    lengths_copy.wait()
    for r in range(row_count):
        key_copy(r).start()
    for r in range(row_count):
        value_copy(r).start()
    queries_copy.wait()
    query[...] = queries[...].astype(f32)
    first_head = pl.multiple_of(lax.axis_index("tensor") * heads_kv, heads_kv)
    first_keys.wait()
    for g, rows in enumerate(groups):
        for r in rows:
            key_copy(r).wait()
        for n in range(g * pieces // group_count, (g + 1) * pieces // group_count):
            weight_copy(n).start()
        for r in rows:
            own = query[r, pl.ds(first_head, heads_kv), :].astype(bf16)
            score = lax.dot_general(own, keys[r], (((1,), (1,)), ((), ())), preferred_element_type=f32)
            slot = lax.broadcasted_iota(jnp.int32, score.shape, 1)
            scores[r * heads_kv : (r + 1) * heads_kv] = jnp.where(slot < lengths[r], score, -1e30)
    totals = []
    for r in range(row_count):
        score = scores[r * heads_kv : (r + 1) * heads_kv]
        top = jnp.max(score, axis=1, keepdims=True)
        mass = jnp.exp((score - top) * (1.0 / depth**0.5))
        totals.append(jnp.sum(mass, axis=1, keepdims=True))
        probs[r] = mass.astype(bf16)
    first_values.wait()
    for rows in groups:
        for r in rows:
            value_copy(r).wait()
        for r in rows:
            mixed = jnp.dot(probs[r], values[r], preferred_element_type=f32)
            heads_out[r * heads_kv : (r + 1) * heads_kv] = mixed / totals[r]
    attended = jnp.concatenate(
        [heads_out[pl.ds(h, row_count, stride=heads_kv), :] for h in range(heads_kv)], axis=1
    ).astype(bf16)
    total = None
    for n in range(pieces):
        weight_copy(n).wait()
        rows = slice(n * piece, (n + 1) * piece)
        term = jnp.dot(attended[:, rows], weight[rows], preferred_element_type=f32)
        total = term if total is None else total + term
    out[...] = total.astype(out.dtype)


def in_hbm(array):
    return pltpu.with_memory_space_constraint(array, pltpu.HBM)


def attend_project(lengths, queries, keys, values, weight):
    row_count, span, depth = keys.shape
    heads_kv = HEADS // KV_HEADS
    pieces = 8
    return pl.pallas_call(
        attend_project_kernel,
        out_shape=pltpu.VMEM((row_count, weight.shape[1]), bf16),
        in_specs=[pl.BlockSpec(memory_space=pl.ANY)] * 5,
        out_specs=pl.BlockSpec(memory_space=pltpu.VMEM),
        scratch_shapes=[
            pltpu.SMEM(lengths.shape, jnp.int32),
            pltpu.VMEM(queries.shape, bf16),
            pltpu.VMEM(keys.shape, bf16),
            pltpu.VMEM(values.shape, bf16),
            pltpu.VMEM(weight.shape, bf16),
            pltpu.VMEM(queries.shape, f32),
            pltpu.VMEM((row_count * heads_kv, span), f32),
            pltpu.VMEM((row_count, heads_kv, span), bf16),
            pltpu.VMEM((row_count * heads_kv, depth), f32),
            pltpu.SemaphoreType.DMA((4,)),
            pltpu.SemaphoreType.DMA((row_count,)),
            pltpu.SemaphoreType.DMA((row_count,)),
            pltpu.SemaphoreType.DMA((pieces,)),
        ],
        compiler_params=pltpu.CompilerParams(vmem_limit_bytes=57 << 20),
        name="attend_project",
    )(in_hbm(lengths), in_hbm(queries), in_hbm(keys), in_hbm(values), in_hbm(weight))


def relay_kernel(source, one, two, target):
    target[...] = source[...]


def relay(source, one, two):
    vmem = pl.BlockSpec(memory_space=pltpu.VMEM)
    return pl.pallas_call(
        relay_kernel,
        out_shape=pltpu.VMEM(source.shape, source.dtype),
        in_specs=[vmem, pl.BlockSpec(memory_space=pl.ANY), pl.BlockSpec(memory_space=pl.ANY)],
        out_specs=vmem,
        compiler_params=pltpu.CompilerParams(vmem_limit_bytes=1 << 20),
        name="relay",
    )(source, in_hbm(one), in_hbm(two))


def head_kernel(part_count, targets, *refs):
    parts = refs[:part_count]
    residual, gain, weight, keep, send, own = refs[part_count:]
    row_count, width = residual.shape
    vocab = weight.shape[1]
    half = row_count // 2
    chunks = 4
    chunk = width // chunks
    square = 0.0
    logits = 0.0
    for n in range(chunks):
        columns = slice(n * chunk, (n + 1) * chunk)
        hidden = residual[:, columns].astype(f32)
        for part in parts:
            hidden = hidden + part[:, columns].astype(f32)
        square = square + jnp.sum(hidden * hidden, axis=1, keepdims=True)
        gained = (hidden * gain[:, columns]).astype(bf16)
        logits = logits + jnp.dot(gained, weight[columns], preferred_element_type=f32)
    logits = logits * lax.rsqrt(square / width + 1e-05)
    row = lax.broadcasted_iota(jnp.int32, (row_count, row_count), 0)
    column = lax.broadcasted_iota(jnp.int32, (row_count, row_count), 1)
    wanted = jnp.sum(jnp.where(row == column, targets[...], 0), axis=1, keepdims=True)
    wanted = wanted - lax.axis_index("tensor") * vocab
    entry = lax.broadcasted_iota(jnp.int32, (row_count, vocab), 1)
    pick = jnp.sum(jnp.where(entry == wanted, logits, 0.0), axis=1, keepdims=True)
    top = jnp.max(logits, axis=1, keepdims=True)
    mass = jnp.sum(jnp.exp(logits - top), axis=1, keepdims=True)
    stats = jnp.concatenate([jnp.broadcast_to(part, (row_count, LANES)) for part in (top, mass, pick)], axis=1)
    own[...] = stats
    second = lax.axis_index("member") == 1
    for lanes, block in ((slice(0, vocab), logits), (slice(vocab, vocab + STAT_LANES), stats)):
        keep[:, lanes] = jnp.where(second, block[half:], block[:half])
        send[:, lanes] = jnp.where(second, block[:half], block[half:])


def head_rows(targets, parts, residual, gain, weight):
    row_count, width = residual.shape
    vocab = weight.shape[1]
    vmem = pl.BlockSpec(memory_space=pltpu.VMEM)
    shape = jax.ShapeDtypeStruct((row_count // 2, vocab + STAT_LANES), f32)
    return pl.pallas_call(
        functools.partial(head_kernel, len(parts)),
        out_shape=(shape, shape, jax.ShapeDtypeStruct((row_count, STAT_LANES), f32)),
        in_specs=[vmem] * (len(parts) + 4),
        out_specs=(vmem, vmem, vmem),
        compiler_params=pltpu.CompilerParams(vmem_limit_bytes=16 << 20),
        name="head_rows",
    )(targets[None, :], *parts, residual, gain, weight)


def finish_kernel(tile_count, across, keep, other, *refs):
    tiles = [ref[...] for ref in refs[:tile_count]]
    mean_out, target_out = refs[-2:]
    half, vocab = mean_out.shape
    if across:
        ours, theirs = (ref[...] for ref in refs[tile_count:-2])
        second = lax.axis_index("member") == 1
        mine = [jnp.where(second, block[half:], block[:half]) for block in (ours, theirs)]
        tiles.append(jnp.concatenate(mine, axis=0))
    tops, masses, picks = ([tile[:, n * LANES : (n + 1) * LANES] for tile in tiles] for n in range(3))
    top = functools.reduce(jnp.maximum, tops)
    mass = sum(part * jnp.exp(own_top - top) for part, own_top in zip(masses, tops))
    pick = sum(picks)
    log_total = top + jnp.log(mass)
    both = log_total[:half] + log_total[half:]
    for start in range(0, vocab, LANES):
        lanes = slice(start, start + LANES)
        mean_out[:, lanes] = 0.5 * ((keep[:, lanes] + other[:, lanes]) - both)
    target = 0.5 * ((pick[:half] + pick[half:]) - both)
    row = lax.broadcasted_iota(jnp.int32, (half, half), 0)
    column = lax.broadcasted_iota(jnp.int32, (half, half), 1)
    target_out[...] = jnp.sum(jnp.where(row == column, target[:, :half], 0.0), axis=0)


def finish(keep, other, tiles, across=()):
    half = keep.shape[0]
    vocab = keep.shape[1] - STAT_LANES
    vmem = pl.BlockSpec(memory_space=pltpu.VMEM)
    return pl.pallas_call(
        functools.partial(finish_kernel, len(tiles), bool(across)),
        out_shape=(jax.ShapeDtypeStruct((half, vocab), f32), jax.ShapeDtypeStruct((half,), f32)),
        in_specs=[vmem] * (2 + len(tiles) + len(across)),
        out_specs=(vmem, vmem),
        compiler_params=pltpu.CompilerParams(vmem_limit_bytes=4 << 20),
        name="finish",
    )(keep, other, *tiles, *across)


def attend_shared(queries, keys, values, lengths, group_size, heads_dev):
    my_rank = lax.axis_index("tensor")
    heads_kv = HEADS // KV_HEADS
    row_count, key_span, head_depth = keys.shape
    kv_index = my_rank // group_size
    slot_first = my_rank % group_size * key_span
    group_query = lax.dynamic_slice_in_dim(queries, kv_index * heads_kv, heads_kv, 1)
    scores = jnp.einsum("rqd,rcd->rqc", group_query, keys, preferred_element_type=jnp.float32)
    scores = scores * (1.0 / head_depth**0.5)
    slot_ids = slot_first + jnp.arange(key_span, dtype=jnp.int32)
    live = (slot_ids[None, :] < lengths[:, None])[:, None, :]
    scores = jnp.where(live, scores, jnp.float32(-1e30))
    top_score = jnp.max(scores, axis=-1)
    weights = jnp.where(live, jnp.exp(scores - top_score[..., None]), jnp.float32(0.0))
    weight_total = jnp.sum(weights, axis=-1)
    weighted = jnp.einsum(
        "rqc,rcd->rqd", weights.astype(jnp.bfloat16), values, preferred_element_type=jnp.float32
    )
    state = (top_score, weight_total, weighted)
    for level in range(group_size.bit_length() - 1):
        partner = swapped(
            (for_sending(state[0]), for_sending(state[1]), for_sending(state[2])), "tensor", level
        )
        state = join_partial(state, partner)
    top_score, weight_total, weighted = state
    head_first = my_rank % group_size * heads_dev
    own_total = lax.dynamic_slice_in_dim(weight_total, head_first, heads_dev, 1)
    own_weighted = lax.dynamic_slice_in_dim(weighted, head_first, heads_dev, 1)
    return (
        (own_weighted / own_total[..., None])
        .reshape(row_count, heads_dev * head_depth)
        .astype(jnp.bfloat16)
    )


def local(queries, keys, values, lengths, targets, residual, out_weight, norm_gain, head_weight):
    axis_width = lax.axis_size("tensor")
    group_size = axis_width // KV_HEADS
    heads_dev = HEADS // axis_width
    direct = axis_width == 4
    if group_size == 1:
        projected = attend_project(lengths, queries[0], keys[0], values[0], out_weight[0])
    else:
        attended = attend_shared(queries[0], keys[0], values[0], lengths, group_size, heads_dev)
        projected = jnp.dot(attended, out_weight[0], preferred_element_type=jnp.float32).astype(bf16)
    if direct:
        again = relay(projected, keys[0], values[0])
        parts = [again] + [crossed(again, "tensor", mask) for mask in range(1, axis_width)]
    else:
        parts = [lax.psum(projected, "tensor")]
    head_local = head_weight[0]
    keep, send, stats = head_rows(targets, parts, residual[0], norm_gain, head_weight[0])
    other = swapped(send, "member", 0)
    vocab = head_weight.shape[2]
    tile = jnp.concatenate([keep[:, vocab:], other[:, vocab:]], axis=0)
    if direct:
        ours = crossed(stats, "tensor", 3)
        tiles = [tile, crossed(tile, "tensor", 1), crossed(tile, "tensor", 2)]
        held, _ = lax.optimization_barrier((ours, tiles[2]))
        return finish(keep, other, tiles, (ours, swapped(held, "member", 0)))
    gathered = lax.all_gather(tile, "tensor")
    return finish(keep, other, [gathered[i] for i in range(axis_width)])


def solution(mesh):
    placed = (
        P("member", "rep", None, None),
        P("member", "rep", "tensor", None),
        P("member", "rep", "tensor", None),
        P("rep"),
        P("rep"),
        P("member", "rep", None),
        P("member", "tensor", None),
        P("member", None),
        P("member", None, "tensor"),
    )
    return jax.shard_map(
        local,
        mesh=mesh,
        in_specs=placed,
        out_specs=(P(("rep", "member"), "tensor"), P(("rep", "member"))),
        check_vma=False,
    )
```

```python
import functools

import jax
import jax.numpy as jnp
from jax import lax
from jax.experimental import pallas as pl
from jax.experimental.pallas import tpu as pltpu
from jax.sharding import PartitionSpec as P

HEADS = 32
KV_HEADS = 4
SLOT_BLOCK = 128
LEAST_LIVE = 256
LANES = 128
STAT_LANES = 2 * LANES
f32 = jnp.float32
bf16 = jnp.bfloat16


def for_sending(shard):

    def short(part):
        return part.astype(jnp.bfloat16) if part.dtype == jnp.float32 else part

    return jax.tree.map(short, shard)


def swapped(block, axis, distance):
    count = lax.axis_size(axis)
    route = []
    for low in range(count):
        high = low | 1 << distance
        if high != low and high < count:
            route += [(low, high), (high, low)]
    return lax.ppermute(block, axis, route)


def crossed(block, axis, mask):
    count = lax.axis_size(axis)
    return lax.ppermute(block, axis, [(i, i ^ mask) for i in range(count)])


def join_partial(earlier, later):
    peak_one, total_one, weighted_one = earlier
    peak_two, total_two, weighted_two = later
    peak_new = jnp.maximum(peak_one, peak_two)
    scale_one = jnp.exp(peak_one - peak_new)
    scale_two = jnp.exp(peak_two - peak_new)
    total_new = total_one * scale_one + total_two * scale_two
    weighted_new = weighted_one * scale_one[..., None] + weighted_two * scale_two[..., None]
    return (peak_new, total_new, weighted_new)


def attend_project_kernel(
    lengths_hbm, queries_hbm, keys_hbm, values_hbm, weight_hbm, out,
    lengths, queries, keys, values, weight, query, scores, probs, heads_out,
    small_sem, key_sem, value_sem, weight_sem,
):
    row_count, span, depth = keys_hbm.shape
    heads_kv = HEADS // KV_HEADS
    pieces = weight_sem.shape[0]
    piece = weight_hbm.shape[0] // pieces
    group_count = 4
    per_group = row_count // group_count
    groups = [range(g * per_group, (g + 1) * per_group) for g in range(group_count)]

    def first_copy(source, target, sem):
        slots = pl.ds(0, LEAST_LIVE)
        return pltpu.make_async_copy(source.at[:, slots], target.at[:, slots], sem)

    def live_copy(source, target, sem, r):
        live = (lengths[r] + (SLOT_BLOCK - 1)) // SLOT_BLOCK * SLOT_BLOCK
        rest = jnp.maximum(live - LEAST_LIVE, SLOT_BLOCK)
        slots = pl.ds(LEAST_LIVE, pl.multiple_of(rest, SLOT_BLOCK))
        return pltpu.make_async_copy(source.at[r, slots], target.at[r, slots], sem.at[r])

    def key_copy(r):
        return live_copy(keys_hbm, keys, key_sem, r)

    def value_copy(r):
        return live_copy(values_hbm, values, value_sem, r)

    def weight_copy(n):
        rows = pl.ds(n * piece, piece)
        return pltpu.make_async_copy(weight_hbm.at[rows], weight.at[rows], weight_sem.at[n])

    lengths_copy = pltpu.make_async_copy(lengths_hbm, lengths, small_sem.at[0])
    queries_copy = pltpu.make_async_copy(queries_hbm, queries, small_sem.at[1])
    first_keys = first_copy(keys_hbm, keys, small_sem.at[2])
    first_values = first_copy(values_hbm, values, small_sem.at[3])
    lengths_copy.start()
    queries_copy.start()
    first_keys.start()
    first_values.start()
    values[:, LEAST_LIVE:] = jnp.zeros((row_count, span - LEAST_LIVE, depth), bf16)
    lengths_copy.wait()
    for r in range(row_count):
        key_copy(r).start()
    for r in range(row_count):
        value_copy(r).start()
    queries_copy.wait()
    query[...] = queries[...].astype(f32)
    first_head = pl.multiple_of(lax.axis_index("tensor") * heads_kv, heads_kv)
    first_keys.wait()
    for g, rows in enumerate(groups):
        for r in rows:
            key_copy(r).wait()
        for n in range(g * pieces // group_count, (g + 1) * pieces // group_count):
            weight_copy(n).start()
        for r in rows:
            own = query[r, pl.ds(first_head, heads_kv), :].astype(bf16)
            score = lax.dot_general(own, keys[r], (((1,), (1,)), ((), ())), preferred_element_type=f32)
            slot = lax.broadcasted_iota(jnp.int32, score.shape, 1)
            scores[r * heads_kv : (r + 1) * heads_kv] = jnp.where(slot < lengths[r], score, -1e30)
    totals = []
    for r in range(row_count):
        score = scores[r * heads_kv : (r + 1) * heads_kv]
        top = jnp.max(score, axis=1, keepdims=True)
        mass = jnp.exp((score - top) * (1.0 / depth**0.5))
        totals.append(jnp.sum(mass, axis=1, keepdims=True))
        probs[r] = mass.astype(bf16)
    first_values.wait()
    for rows in groups:
        for r in rows:
            value_copy(r).wait()
        for r in rows:
            mixed = jnp.dot(probs[r], values[r], preferred_element_type=f32)
            heads_out[r * heads_kv : (r + 1) * heads_kv] = mixed / totals[r]
    attended = jnp.concatenate(
        [heads_out[pl.ds(h, row_count, stride=heads_kv), :] for h in range(heads_kv)], axis=1
    ).astype(bf16)
    total = None
    for n in range(pieces):
        weight_copy(n).wait()
        rows = slice(n * piece, (n + 1) * piece)
        term = jnp.dot(attended[:, rows], weight[rows], preferred_element_type=f32)
        total = term if total is None else total + term
    out[...] = total.astype(out.dtype)


def in_hbm(array):
    return pltpu.with_memory_space_constraint(array, pltpu.HBM)


def attend_project(lengths, queries, keys, values, weight):
    row_count, span, depth = keys.shape
    heads_kv = HEADS // KV_HEADS
    pieces = 8
    return pl.pallas_call(
        attend_project_kernel,
        out_shape=pltpu.VMEM((row_count, weight.shape[1]), bf16),
        in_specs=[pl.BlockSpec(memory_space=pl.ANY)] * 5,
        out_specs=pl.BlockSpec(memory_space=pltpu.VMEM),
        scratch_shapes=[
            pltpu.SMEM(lengths.shape, jnp.int32),
            pltpu.VMEM(queries.shape, bf16),
            pltpu.VMEM(keys.shape, bf16),
            pltpu.VMEM(values.shape, bf16),
            pltpu.VMEM(weight.shape, bf16),
            pltpu.VMEM(queries.shape, f32),
            pltpu.VMEM((row_count * heads_kv, span), f32),
            pltpu.VMEM((row_count, heads_kv, span), bf16),
            pltpu.VMEM((row_count * heads_kv, depth), f32),
            pltpu.SemaphoreType.DMA((4,)),
            pltpu.SemaphoreType.DMA((row_count,)),
            pltpu.SemaphoreType.DMA((row_count,)),
            pltpu.SemaphoreType.DMA((pieces,)),
        ],
        compiler_params=pltpu.CompilerParams(vmem_limit_bytes=57 << 20),
        name="attend_project",
    )(in_hbm(lengths), in_hbm(queries), in_hbm(keys), in_hbm(values), in_hbm(weight))


def relay_kernel(source, one, two, target):
    target[...] = source[...]


def relay(source, one, two):
    vmem = pl.BlockSpec(memory_space=pltpu.VMEM)
    return pl.pallas_call(
        relay_kernel,
        out_shape=pltpu.VMEM(source.shape, source.dtype),
        in_specs=[vmem, pl.BlockSpec(memory_space=pl.ANY), pl.BlockSpec(memory_space=pl.ANY)],
        out_specs=vmem,
        compiler_params=pltpu.CompilerParams(vmem_limit_bytes=1 << 20),
        name="relay",
    )(source, in_hbm(one), in_hbm(two))


def head_kernel(part_count, targets, *refs):
    parts = refs[:part_count]
    residual, gain, weight, keep, send, own = refs[part_count:]
    row_count, width = residual.shape
    vocab = weight.shape[1]
    half = row_count // 2
    chunks = 4
    chunk = width // chunks
    square = 0.0
    logits = 0.0
    for n in range(chunks):
        columns = slice(n * chunk, (n + 1) * chunk)
        hidden = residual[:, columns].astype(f32)
        for part in parts:
            hidden = hidden + part[:, columns].astype(f32)
        square = square + jnp.sum(hidden * hidden, axis=1, keepdims=True)
        gained = (hidden * gain[:, columns]).astype(bf16)
        logits = logits + jnp.dot(gained, weight[columns], preferred_element_type=f32)
    logits = logits * lax.rsqrt(square / width + 1e-05)
    row = lax.broadcasted_iota(jnp.int32, (row_count, row_count), 0)
    column = lax.broadcasted_iota(jnp.int32, (row_count, row_count), 1)
    wanted = jnp.sum(jnp.where(row == column, targets[...], 0), axis=1, keepdims=True)
    wanted = wanted - lax.axis_index("tensor") * vocab
    entry = lax.broadcasted_iota(jnp.int32, (row_count, vocab), 1)
    pick = jnp.sum(jnp.where(entry == wanted, logits, 0.0), axis=1, keepdims=True)
    top = jnp.max(logits, axis=1, keepdims=True)
    mass = jnp.sum(jnp.exp(logits - top), axis=1, keepdims=True)
    stats = jnp.concatenate([jnp.broadcast_to(part, (row_count, LANES)) for part in (top + jnp.log(mass), pick)], axis=1)
    own[...] = stats
    second = lax.axis_index("member") == 1
    for lanes, block in ((slice(0, vocab), logits), (slice(vocab, vocab + STAT_LANES), stats)):
        keep[:, lanes] = jnp.where(second, block[half:], block[:half])
        send[:, lanes] = jnp.where(second, block[:half], block[half:])


def head_rows(targets, parts, residual, gain, weight):
    row_count, width = residual.shape
    vocab = weight.shape[1]
    vmem = pl.BlockSpec(memory_space=pltpu.VMEM)
    shape = jax.ShapeDtypeStruct((row_count // 2, vocab + STAT_LANES), f32)
    return pl.pallas_call(
        functools.partial(head_kernel, len(parts)),
        out_shape=(shape, shape, jax.ShapeDtypeStruct((row_count, STAT_LANES), f32)),
        in_specs=[vmem] * (len(parts) + 4),
        out_specs=(vmem, vmem, vmem),
        compiler_params=pltpu.CompilerParams(vmem_limit_bytes=16 << 20),
        name="head_rows",
    )(targets[None, :], *parts, residual, gain, weight)


def finish_kernel(tile_count, across, keep, other, *refs):
    tiles = [ref[...] for ref in refs[:tile_count]]
    mean_out, target_out = refs[-2:]
    half, vocab = mean_out.shape
    if across:
        ours, theirs = (ref[...] for ref in refs[tile_count:-2])
        second = lax.axis_index("member") == 1
        mine = [jnp.where(second, block[half:], block[:half]) for block in (ours, theirs)]
        tiles.append(jnp.concatenate(mine, axis=0))
    parts, picks = ([tile[:, n * LANES : (n + 1) * LANES] for tile in tiles] for n in range(2))
    top = functools.reduce(jnp.maximum, parts)
    mass = sum(jnp.exp(part - top) for part in parts)
    pick = sum(picks)
    log_total = top + jnp.log(mass)
    both = log_total[:half] + log_total[half:]
    for start in range(0, vocab, LANES):
        lanes = slice(start, start + LANES)
        mean_out[:, lanes] = 0.5 * ((keep[:, lanes] + other[:, lanes]) - both)
    target = 0.5 * ((pick[:half] + pick[half:]) - both)
    row = lax.broadcasted_iota(jnp.int32, (half, half), 0)
    column = lax.broadcasted_iota(jnp.int32, (half, half), 1)
    target_out[...] = jnp.sum(jnp.where(row == column, target[:, :half], 0.0), axis=0)


def finish(keep, other, tiles, across=()):
    half = keep.shape[0]
    vocab = keep.shape[1] - STAT_LANES
    vmem = pl.BlockSpec(memory_space=pltpu.VMEM)
    return pl.pallas_call(
        functools.partial(finish_kernel, len(tiles), bool(across)),
        out_shape=(jax.ShapeDtypeStruct((half, vocab), f32), jax.ShapeDtypeStruct((half,), f32)),
        in_specs=[vmem] * (2 + len(tiles) + len(across)),
        out_specs=(vmem, vmem),
        compiler_params=pltpu.CompilerParams(vmem_limit_bytes=4 << 20),
        name="finish",
    )(keep, other, *tiles, *across)


def attend_shared(queries, keys, values, lengths, group_size, heads_dev):
    my_rank = lax.axis_index("tensor")
    heads_kv = HEADS // KV_HEADS
    row_count, key_span, head_depth = keys.shape
    kv_index = my_rank // group_size
    slot_first = my_rank % group_size * key_span
    group_query = lax.dynamic_slice_in_dim(queries, kv_index * heads_kv, heads_kv, 1)
    scores = jnp.einsum("rqd,rcd->rqc", group_query, keys, preferred_element_type=jnp.float32)
    scores = scores * (1.0 / head_depth**0.5)
    slot_ids = slot_first + jnp.arange(key_span, dtype=jnp.int32)
    live = (slot_ids[None, :] < lengths[:, None])[:, None, :]
    scores = jnp.where(live, scores, jnp.float32(-1e30))
    top_score = jnp.max(scores, axis=-1)
    weights = jnp.where(live, jnp.exp(scores - top_score[..., None]), jnp.float32(0.0))
    weight_total = jnp.sum(weights, axis=-1)
    weighted = jnp.einsum(
        "rqc,rcd->rqd", weights.astype(jnp.bfloat16), values, preferred_element_type=jnp.float32
    )
    state = (top_score, weight_total, weighted)
    for level in range(group_size.bit_length() - 1):
        partner = swapped(
            (for_sending(state[0]), for_sending(state[1]), for_sending(state[2])), "tensor", level
        )
        state = join_partial(state, partner)
    top_score, weight_total, weighted = state
    head_first = my_rank % group_size * heads_dev
    own_total = lax.dynamic_slice_in_dim(weight_total, head_first, heads_dev, 1)
    own_weighted = lax.dynamic_slice_in_dim(weighted, head_first, heads_dev, 1)
    return (
        (own_weighted / own_total[..., None])
        .reshape(row_count, heads_dev * head_depth)
        .astype(jnp.bfloat16)
    )


def local(queries, keys, values, lengths, targets, residual, out_weight, norm_gain, head_weight):
    axis_width = lax.axis_size("tensor")
    group_size = axis_width // KV_HEADS
    heads_dev = HEADS // axis_width
    direct = axis_width == 4
    if group_size == 1:
        projected = attend_project(lengths, queries[0], keys[0], values[0], out_weight[0])
    else:
        attended = attend_shared(queries[0], keys[0], values[0], lengths, group_size, heads_dev)
        projected = jnp.dot(attended, out_weight[0], preferred_element_type=jnp.float32).astype(bf16)
    if direct:
        again = relay(projected, keys[0], values[0])
        parts = [again] + [crossed(again, "tensor", mask) for mask in range(1, axis_width)]
    else:
        parts = [lax.psum(projected, "tensor")]
    head_local = head_weight[0]
    keep, send, stats = head_rows(targets, parts, residual[0], norm_gain, head_weight[0])
    other = swapped(send, "member", 0)
    vocab = head_weight.shape[2]
    tile = jnp.concatenate([keep[:, vocab:], other[:, vocab:]], axis=0)
    if direct:
        ours = crossed(stats, "tensor", 3)
        tiles = [tile, crossed(tile, "tensor", 1), crossed(tile, "tensor", 2)]
        held, _ = lax.optimization_barrier((ours, tiles[2]))
        return finish(keep, other, tiles, (ours, swapped(held, "member", 0)))
    gathered = lax.all_gather(tile, "tensor")
    return finish(keep, other, [gathered[i] for i in range(axis_width)])


def solution(mesh):
    placed = (
        P("member", "rep", None, None),
        P("member", "rep", "tensor", None),
        P("member", "rep", "tensor", None),
        P("rep"),
        P("rep"),
        P("member", "rep", None),
        P("member", "tensor", None),
        P("member", None),
        P("member", None, "tensor"),
    )
    return jax.shard_map(
        local,
        mesh=mesh,
        in_specs=placed,
        out_specs=(P(("rep", "member"), "tensor"), P(("rep", "member"))),
        check_vma=False,
    )
```
